128 devices in a mesh: tm: 8 (over x, core), col: 16 (over z, y).
Axes of the slice: x: 4, y: 4, z: 4, core: 2. Of those that a mesh axis runs over, the one named last changes fastest.
Arguments:
- interior: float32 [8, 2048, 2048], P('tm', None, 'col'), may hold values from -1 to 10, as said below
- left_coupling: float32 [8, 2048, 2048], P('tm', None, 'col'), may hold values from -0.25 to 0.25
- right_coupling: float32 [8, 2048, 2048], P('tm', None, 'col'), may hold values from -0.25 to 0.25
- effects_rows: float32 [8, 64, 2048], P('tm'), may hold values from -0.25 to 0.25
- separator: float32 [8, 2048, 2048], P('tm', None, 'col'), may hold values from -6 to 6
- separator_effects: float32 [8, 64, 2048], P('tm', None, 'col'), may hold values from -1.5 to 1.5
- effects_tip: float32 [64, 64], replicated, may hold values from -6 to 6
Outputs:
- factor: float32 [8, 2048, 2048], P('tm', None, 'col')
- separator_diagonal: float32 [8, 2048, 2048], P('tm', None, 'col')
- separator_coupling: float32 [8, 2048, 2048], P('tm', None, 'col')
- separator_arrow: float32 [8, 64, 2048], P('tm', None, 'col')
- updated_tip: float32 [64, 64], replicated
The draws below stay inside these ranges and needn't reach their ends.
Inputs may be any that keep to these rules, and one draw needn't show every extreme that they name: Each interior block is symmetric with diagonal entries of 3 or more and a small off-diagonal part, so it is positive definite.
All inputs are finite; a program needn't handle non-finite values.
Results may differ from the reference program's by a relative error of at most 0.000073.
Values sent between devices are 32-bit elements; how exact they have to be, the bound alone decides.
A program may use at most 192 MiB of HBM per device.

```python
import math
import jax
import jax.numpy as jnp
from jax import lax

B = 2048
NF = 64
TBLOCKS = 8


def draw_interior(key, part):
    key = jax.random.fold_in(key, 11)
    first_key, second_key = jax.random.split(key)
    rough = jax.random.uniform(first_key, (TBLOCKS, B, B), jnp.float32, -1.0, 1.0)
    symmetric = (rough + jnp.swapaxes(rough, 1, 2)) * (0.9 * math.sqrt(1.5) / math.sqrt(B))
    identity = jnp.eye(B, dtype=jnp.float32)
    symmetric = symmetric * (1.0 - identity)
    highest = 6.0
    diagonal = jnp.exp(jax.random.uniform(second_key, (TBLOCKS, B), jnp.float32, math.log(3.0), math.log(highest)))
    return symmetric + diagonal[:, :, None] * identity


def shard_levels(rng, extent, cuts, smallest, largest):
    loudness, own = 1.0, jax.random.fold_in(rng, 6)
    for axis_at, shards_of in cuts:
        heights = jnp.exp(jax.random.uniform(jax.random.fold_in(own, axis_at), (shards_of,), jnp.float32, smallest / len(cuts), largest / len(cuts)))
        loudness = loudness * jnp.repeat(heights, extent[axis_at] // shards_of).reshape([-1 if axis == axis_at else 1 for axis in range(len(extent))])
    return loudness


def scatter_about(key, extent, scale, reach, pieces=(), kind=jnp.bfloat16):
    result = scale * jax.random.normal(key, extent, jnp.float32)
    if pieces:
        result = result * shard_levels(key, extent, pieces, -0.22, 0.18)
    return jnp.clip(result, -reach, reach).astype(kind)


def setup_inputs(seed: int = 0) -> dict:
    splits = jax.random.split(jax.random.key(seed), 8)
    return {
        "interior": draw_interior(jax.random.fold_in(splits[7], 71), 0),
        "left_coupling": scatter_about(splits[1], (TBLOCKS, B, B), (B // 4) ** -0.5, 0.25, ((0, 8), (2, 16)), jnp.float32),
        "right_coupling": scatter_about(splits[2], (TBLOCKS, B, B), (B // 4) ** -0.5, 0.25, ((0, 8), (2, 16)), jnp.float32),
        "effects_rows": scatter_about(splits[3], (TBLOCKS, NF, B), (B // 4) ** -0.5, 0.25, ((0, 8),), jnp.float32),
        "separator": scatter_about(splits[4], (TBLOCKS, B, B), 1.0, 6.0, ((0, 8), (2, 16)), jnp.float32),
        "separator_effects": scatter_about(splits[5], (TBLOCKS, NF, B), 0.1, 1.5, ((0, 8), (2, 16)), jnp.float32),
        "effects_tip": scatter_about(splits[6], (NF, NF), 1.0, 6.0, (), jnp.float32),
    }


def product(left, right):
    return jnp.dot(left.astype(jnp.float32), right.astype(jnp.float32), precision=lax.Precision.HIGHEST, preferred_element_type=jnp.float32)

def partition(blocks):
    interior, left_coupling, right_coupling, effects_rows = blocks
    factor = jnp.linalg.cholesky(interior)
    solving = jnp.concatenate([left_coupling, right_coupling, effects_rows.T], axis=1)
    solved = lax.linalg.triangular_solve(factor, solving, left_side=True, lower=True)
    left_solved = solved[:, :B]
    right_solved = solved[:, B:2 * B]
    effects_solved = solved[:, 2 * B:]
    left_gram = product(left_solved.T, left_solved)
    right_gram = product(right_solved.T, right_solved)
    cross_gram = product(left_solved.T, right_solved)
    effects_gram = product(effects_solved.T, effects_solved)
    right_cross = product(effects_solved.T, right_solved)
    left_cross = product(effects_solved.T, left_solved)
    return (factor, left_gram, right_gram, cross_gram, effects_gram, right_cross, left_cross)

def reference(interior, left_coupling, right_coupling, effects_rows, separator, separator_effects, effects_tip):
    outputs = lax.map(partition, (interior, left_coupling, right_coupling, effects_rows))
    factor, left_gram, right_gram, cross_gram, effects_gram, right_cross, left_cross = outputs
    next_gram = jnp.concatenate([left_gram[1:], jnp.zeros((1, B, B), jnp.float32)], axis=0)
    next_cross = jnp.concatenate([left_cross[1:], jnp.zeros((1, NF, B), jnp.float32)], axis=0)
    separator_diagonal = separator - right_gram - next_gram
    separator_coupling = -cross_gram
    separator_arrow = separator_effects - right_cross - next_cross
    updated_tip = effects_tip - jnp.sum(effects_gram, axis=0)
    return (factor, separator_diagonal, separator_coupling, separator_arrow, updated_tip)
```

```python
import jax
import jax.numpy as jnp
from jax import lax
from jax.experimental import pallas as pl
from jax.experimental.pallas import tpu as pltpu
from jax.sharding import PartitionSpec as P

W = 128
N = 16
B = N * W
NF = 64
X0 = B
XW = 3 * W
TILES = N * (N + 1) // 2
MESH = pl.DeviceIdType.MESH
F32, BF16 = jnp.float32, jnp.bfloat16
OFFSETS = ((0, 1), (1, 0), (3, 3), (3, 1), (1, 2), (2, 3), (0, 2), (2, 0), (2, 2))
FULL = 6


def split(x):
    high = x.astype(BF16)
    return high, (x - high.astype(F32)).astype(BF16)


def dot3(a_high, a_low, b_high, b_low):
    def one(a, b):
        return jnp.dot(a, b, preferred_element_type=F32)

    return one(a_high, b_high) + (one(a_high, b_low) + one(a_low, b_high))


def corner(rows):
    lane = lax.broadcasted_iota(jnp.int32, (8, W), 1)
    sub = lax.broadcasted_iota(jnp.int32, (8, W), 0)
    first = lane[0:1]
    rows = list(rows)
    upper, inverse = [], []

    def lanes(x, c):
        return jnp.broadcast_to(x[:, c : c + 1], (8, W))

    for s in range(W // 8):
        r = 8 * s
        block = rows[s]
        c = [lanes(block, r + j) for j in range(8)]
        e = {(i, j): c[j][i : i + 1, :] for j in range(8) for i in range(j, 8)}
        inv, low = [None] * 8, {}
        for j in range(8):
            inv[j] = lax.rsqrt(e[j, j])
            for i in range(j + 1, 8):
                low[i, j] = e[i, j] * inv[j]
            for i in range(j + 1, 8):
                for m in range(j + 1, i + 1):
                    e[i, m] = e[i, m] - low[i, j] * low[m, j]
        diagonal = (lane >= r) & (lane < r + 8)
        own = jnp.where(diagonal, (lane - r == sub).astype(F32), block)
        u = []
        for j in range(8):
            t = own[j : j + 1, :]
            for m in range(j):
                t = t - low[j, m] * u[m]
            u.append(t * inv[j])
        z = [None] * 8
        for j in reversed(range(8)):
            t = u[j]
            for m in range(j + 1, 8):
                t = t - low[m, j] * z[m]
            z[j] = t * inv[j]
        solved = jnp.concatenate(u, axis=0)
        small = jnp.zeros((8, W), F32)
        for j in range(8):
            t = jnp.where(first == r + j, e[j, j] * inv[j], 0.0)
            for m in range(j + 1, 8):
                t = jnp.where(first == r + m, low[m, j], t)
            small = jnp.where(sub == j, t, small)
        upper.append(jnp.where(lane >= r + 8, solved, small))
        inverse.append(jnp.where(lane < r + 8, solved, 0.0))
        z = [jnp.broadcast_to(t, (8, W)) for t in z]
        for i in range(s + 1, W // 8):
            t = jnp.where(diagonal, 0.0, rows[i])
            for j in range(8):
                t = t - lanes(rows[i], r + j) * z[j]
            rows[i] = t
    return upper, inverse


def tile(k, j):
    return k * (2 * N + 1 - k) // 2 + j - k


def at(i, size=W):
    return pl.ds(pl.multiple_of(i * size, size), size)


def kernel(
    a, left, right, effects, separator, separator_effects, tip,
    factor, diagonal_out, coupling_out, arrow_out, tip_out,
    tiles, high, low, panel, corner_up, corner_inv, x_own, x_got, xt_high, xt_low, self_gram,
    result_got, next_got, cross_got, tip_got, tip_own, cross_own,
    tile_send, tile_recv, x_send, x_recv, result_send, result_recv,
    next_send, next_recv, cross_send, cross_recv, tip_send, tip_recv,
):
    me = lax.axis_index("col")
    tm = lax.axis_index("tm")
    tms = lax.axis_size("tm")
    z, y = me // 4, me % 4

    def moved(dz, dy):
        return ((z + dz + 4) % 4) * 4 + (y + dy + 4) % 4

    barrier = pltpu.get_barrier_semaphore()

    def greet(o, _):
        pl.semaphore_signal(barrier, inc=1, device_id={"tm": tm, "col": (me + o) % N}, device_id_type=MESH)
        return 0

    lax.fori_loop(1, N, greet, 0)

    def greet_tm(o, _):
        pl.semaphore_signal(barrier, inc=1, device_id={"tm": (tm + o) % tms, "col": me}, device_id_type=MESH)
        return 0

    lax.fori_loop(1, tms, greet_tm, 0)
    pl.semaphore_wait(barrier, N - 1 + tms - 1)

    def tile_copy(k, o):
        to = ((z + o // 4) % 4) * 4 + (y + o % 4) % 4
        return pltpu.make_async_remote_copy(
            src_ref=a.at[at(k)], dst_ref=tiles.at[tile(k, me)],
            send_sem=tile_send.at[k, o], recv_sem=tile_recv.at[tile(k, me)],
            device_id={"tm": tm, "col": to}, device_id_type=MESH,
        )

    def tile_arrival(k, j):
        return pltpu.make_async_remote_copy(
            src_ref=a.at[at(k)], dst_ref=tiles.at[tile(k, j)],
            send_sem=tile_send.at[k, 1], recv_sem=tile_recv.at[tile(k, j)],
            device_id={"tm": tm, "col": (me + 1) % N}, device_id_type=MESH,
        )

    def send_tiles(k, _):
        def to_one(o, _):
            tile_copy(k, o).start()
            return 0

        lax.fori_loop(1, N, to_one, 0)
        tiles[tile(k, me)] = a[at(k), :]
        return 0

    lax.fori_loop(0, me + 1, send_tiles, 0)

    def clear(k, _):
        high[at(k), :] = jnp.zeros((W, B + XW), BF16)
        low[at(k), :] = jnp.zeros((W, B + XW), BF16)
        factor[at(k), :] = jnp.zeros((W, W), F32)
        return 0

    lax.fori_loop(0, N, clear, 0)

    own_bit = (y // 2, z // 2, z // 2)

    def slot(d, k):
        return d * N + k if d < FULL else FULL * N + (d - FULL) * (N // 2) + k // 2

    def x_copy(d, k):
        return pltpu.make_async_remote_copy(
            src_ref=x_own.at[at(k)], dst_ref=x_got.at[slot(d, k)],
            send_sem=x_send.at[slot(d, k)], recv_sem=x_recv.at[slot(d, k)],
            device_id={"tm": tm, "col": moved(*OFFSETS[d])}, device_id_type=MESH,
        )

    def updated(k, begin, width):
        def add(kk, total):
            return total + dot3(
                high[at(k), at(kk, 2 * W)], low[at(k), at(kk, 2 * W)],
                high[at(kk, 2 * W), pl.ds(begin, width)], low[at(kk, 2 * W), pl.ds(begin, width)],
            )

        return lax.fori_loop(0, (k + 1) // 2, add, jnp.zeros((W, width), F32))

    def step(k, _):
        def wait_tile(j, _):
            @pl.when(j != me)
            def _():
                tile_arrival(k, j).wait_recv()

            return 0

        lax.fori_loop(k, N, wait_tile, 0)

        def update_four(c, _):
            begin = pl.multiple_of(c * 4 * W, 4 * W)
            total = updated(k, begin, 4 * W)
            for i in range(4):
                j = c * 4 + i

                @pl.when(j >= k)
                def _():
                    panel[:, at(j)] = tiles[tile(k, jnp.maximum(j, k))] - total[:, i * W : (i + 1) * W]

            return 0

        lax.fori_loop(k // 4, N // 4, update_four, 0)
        total = updated(k, X0, XW)
        panel[:, X0 : X0 + W] = left[at(k), :] - total[:, :W]
        panel[:, X0 + W : X0 + 2 * W] = right[at(k), :] - total[:, W : 2 * W]
        rows = jnp.concatenate([effects[:, at(k)], jnp.zeros((W - NF, W), F32)], axis=0)
        panel[:, X0 + 2 * W :] = rows.T - total[:, 2 * W :]

        upper, inverse = corner([panel[8 * i : 8 * i + 8, at(k)] for i in range(W // 8)])
        for i in range(W // 8):
            corner_up[8 * i : 8 * i + 8, :] = upper[i]
            corner_inv[8 * i : 8 * i + 8, :] = inverse[i]

        @pl.when(me == k)
        def _():
            factor[at(k), :] = corner_up[...].T

        inv_high, inv_low = split(corner_inv[...])

        def solve_four(c, _):
            begin = pl.multiple_of(c * 4 * W, 4 * W)
            part = dot3(inv_high, inv_low, *split(panel[:, pl.ds(begin, 4 * W)]))
            for i in range(4):
                j = c * 4 + i

                @pl.when(j > k)
                def _():
                    one = part[:, i * W : (i + 1) * W]
                    high[at(k), at(j)], low[at(k), at(j)] = split(one)
                    turned = one.T
                    high[at(j), at(k)], low[at(j), at(k)] = split(turned)

                    @pl.when(me == k)
                    def _():
                        factor[at(j), :] = turned

            return 0

        lax.fori_loop(k // 4, N // 4, solve_four, 0)
        part = dot3(inv_high, inv_low, *split(panel[:, X0:]))
        x_own[at(k), :] = part[:, : 2 * W]
        high[at(k), X0:], low[at(k), X0:] = split(part)
        for i in range(3):
            rows = slice(i * W, (i + 1) * W)
            xt_high[rows, at(k)], xt_low[rows, at(k)] = split(part[:, rows].T)
        for d in range(len(OFFSETS)):
            if d < FULL:
                x_copy(d, k).start()
            else:

                @pl.when((k + own_bit[d - FULL]) % 2 == 0)
                def _():
                    x_copy(d, k).start()

        return 0

    lax.fori_loop(0, N, step, 0)

    self_gram[...] = jnp.zeros((XW, XW), F32)

    def clear_gram(i, _):
        tiles[i] = jnp.zeros((W, W), F32)
        return 0

    lax.fori_loop(0, 4 * len(OFFSETS), clear_gram, 0)

    def add_gram(d, k, got):
        part = dot3(xt_high[: 2 * W, k], xt_low[: 2 * W, k], *split(got))
        tiles[4 * d] += part[:W, :W]
        tiles[4 * d + 1] += part[:W, W:]
        tiles[4 * d + 2] += part[W:, W:]
        tiles[4 * d + 3] += part[W:, :W]

    def gram_step(p, _):
        pair = at(p, 2 * W)
        self_gram[...] += dot3(xt_high[:, pair], xt_low[:, pair], high[pair, X0:], low[pair, X0:])
        for d in range(len(OFFSETS)):
            if d < FULL:
                x_copy(d, 2 * p).wait_recv()
                x_copy(d, 2 * p + 1).wait_recv()
                got = x_got[pl.ds(d * N + 2 * p, 2)].reshape(2 * W, 2 * W)
                add_gram(d, pair, got)
            else:
                k = 2 * p + 1 - own_bit[d - FULL]
                x_copy(d, k).wait_recv()
                add_gram(d, at(k), x_got[slot(d, k)])
        return 0

    lax.fori_loop(0, N // 2, gram_step, 0)

    def result_copy(d):
        dz, dy = OFFSETS[d]
        return pltpu.make_async_remote_copy(
            src_ref=tiles.at[pl.ds(4 * d, 3)], dst_ref=result_got.at[d],
            send_sem=result_send.at[d], recv_sem=result_recv.at[d],
            device_id={"tm": tm, "col": moved(-dz, -dy)}, device_id_type=MESH,
        )

    for d in range(len(OFFSETS)):
        result_copy(d).start()

    cross_own[...] = self_gram[2 * W : 2 * W + NF, :W]
    tip_own[...] = self_gram[2 * W : 2 * W + NF, 2 * W :]

    def tip_copy(o):
        return pltpu.make_async_remote_copy(
            src_ref=tip_own, dst_ref=tip_got.at[o],
            send_sem=tip_send.at[o], recv_sem=tip_recv.at[o],
            device_id={"tm": (tm + o) % tms, "col": me}, device_id_type=MESH,
        )

    for o in range(1, tms):
        tip_copy(o).start()

    back = {"tm": (tm + tms - 1) % tms, "col": me}
    cross_copy = pltpu.make_async_remote_copy(
        src_ref=cross_own, dst_ref=cross_got, send_sem=cross_send, recv_sem=cross_recv,
        device_id=back, device_id_type=MESH,
    )

    @pl.when(tm > 0)
    def _():
        cross_copy.start()

    base = 4 * len(OFFSETS)

    def next_copy(b):
        return pltpu.make_async_remote_copy(
            src_ref=tiles.at[base + b], dst_ref=next_got.at[b],
            send_sem=next_send.at[b], recv_sem=next_recv.at[b],
            device_id=back, device_id_type=MESH,
        )

    def block_out(b, left_gram, cross_gram, right_gram):
        tiles[base + b] = left_gram

        @pl.when(tm > 0)
        def _():
            next_copy(b).start()

        coupling_out[at(b), :] = -cross_gram
        diagonal_out[at(b), :] = separator[at(b), :] - right_gram

    block_out(me, self_gram[:W, :W], self_gram[:W, W : 2 * W], self_gram[W : 2 * W, W : 2 * W])
    for d in range(FULL):
        dz, dy = OFFSETS[d]
        block_out(moved(-dz, -dy), tiles[4 * d].T, tiles[4 * d + 3].T, tiles[4 * d + 2].T)
    for d in range(len(OFFSETS)):
        result_copy(d).wait_recv()
        got = [result_got[d, i] for i in range(3)]
        if d >= FULL:
            got = [got[0] + tiles[4 * d].T, got[1] + tiles[4 * d + 3].T, got[2] + tiles[4 * d + 2].T]
        block_out(moved(*OFFSETS[d]), *got)

    total = self_gram[2 * W : 2 * W + NF, 2 * W :]
    for o in range(1, tms):
        tip_copy(o).wait_recv()
        total = total + tip_got[o]
    tip_out[...] = tip[...] - total[:, :NF]

    arrow_out[...] = separator_effects[...] - self_gram[2 * W : 2 * W + NF, W : 2 * W]

    @pl.when(tm < tms - 1)
    def _():
        cross_copy.wait_recv()
        arrow_out[...] -= cross_got[...]

        def add_next(b, _):
            next_copy(b).wait_recv()
            diagonal_out[at(b), :] -= next_got[b]
            return 0

        lax.fori_loop(0, N, add_next, 0)

    def drain_tiles(k, _):
        def one(o, _):
            tile_copy(k, o).wait_send()
            return 0

        lax.fori_loop(1, N, one, 0)
        return 0

    lax.fori_loop(0, me + 1, drain_tiles, 0)
    for d in range(len(OFFSETS)):
        if d < FULL:

            def drain_x(k, _):
                x_copy(d, k).wait_send()
                return 0

            lax.fori_loop(0, N, drain_x, 0)
        else:

            def drain_half(p, _):
                x_copy(d, 2 * p + own_bit[d - FULL]).wait_send()
                return 0

            lax.fori_loop(0, N // 2, drain_half, 0)
        result_copy(d).wait_send()
    for o in range(1, tms):
        tip_copy(o).wait_send()

    @pl.when(tm > 0)
    def _():
        cross_copy.wait_send()

        def drain_next(b, _):
            next_copy(b).wait_send()
            return 0

        lax.fori_loop(0, N, drain_next, 0)


def local(interior, left, right, effects, separator, separator_effects, tip):
    tms = lax.axis_size("tm")
    dma = pltpu.SemaphoreType.DMA
    copies = FULL * N + 3 * (N // 2)
    vmem = pl.BlockSpec(memory_space=pltpu.VMEM)
    outputs = pl.pallas_call(
        kernel,
        out_shape=(
            jax.ShapeDtypeStruct((B, W), F32),
            jax.ShapeDtypeStruct((B, W), F32),
            jax.ShapeDtypeStruct((B, W), F32),
            jax.ShapeDtypeStruct((NF, W), F32),
            jax.ShapeDtypeStruct((NF, NF), F32),
        ),
        in_specs=[vmem] * 7,
        out_specs=[vmem] * 5,
        scratch_shapes=[
            pltpu.VMEM((TILES, W, W), F32),
            pltpu.VMEM((B, B + XW), BF16),
            pltpu.VMEM((B, B + XW), BF16),
            pltpu.VMEM((W, B + XW), F32),
            pltpu.VMEM((W, W), F32),
            pltpu.VMEM((W, W), F32),
            pltpu.VMEM((B, 2 * W), F32),
            pltpu.VMEM((copies, W, 2 * W), F32),
            pltpu.VMEM((XW, B), BF16),
            pltpu.VMEM((XW, B), BF16),
            pltpu.VMEM((XW, XW), F32),
            pltpu.VMEM((len(OFFSETS), 3, W, W), F32),
            pltpu.VMEM((N, W, W), F32),
            pltpu.VMEM((NF, W), F32),
            pltpu.VMEM((8, NF, W), F32),
            pltpu.VMEM((NF, W), F32),
            pltpu.VMEM((NF, W), F32),
            dma((N, N)),
            dma((TILES,)),
            dma((copies,)),
            dma((copies,)),
            dma((len(OFFSETS),)),
            dma((len(OFFSETS),)),
            dma((N,)),
            dma((N,)),
            dma(()),
            dma(()),
            dma((8,)),
            dma((8,)),
        ],
        compiler_params=pltpu.CompilerParams(
            collective_id=0, has_side_effects=True, vmem_limit_bytes=64 * 1024 * 1024 - 65536
        ),
        name="eliminate",
    )(interior[0], left[0], right[0], effects[0], separator[0], separator_effects[0], tip)
    return tuple(x[None] for x in outputs[:4]) + (outputs[4],)


def solution(mesh):
    return jax.shard_map(
        local,
        mesh=mesh,
        in_specs=(
            P("tm", None, "col"),
            P("tm", None, "col"),
            P("tm", None, "col"),
            P("tm", None, None),
            P("tm", None, "col"),
            P("tm", None, "col"),
            P(),
        ),
        out_specs=(
            P("tm", None, "col"),
            P("tm", None, "col"),
            P("tm", None, "col"),
            P("tm", None, "col"),
            P(),
        ),
        check_vma=False,
    )
```

```python
import jax
import jax.numpy as jnp
from jax import lax
from jax.experimental import pallas as pl
from jax.experimental.pallas import tpu as pltpu
from jax.sharding import PartitionSpec as P

W = 128
N = 16
B = N * W
NF = 64
X0 = B
XW = 3 * W
TILES = N * (N + 1) // 2
MESH = pl.DeviceIdType.MESH
F32, BF16 = jnp.float32, jnp.bfloat16
OFFSETS = ((0, 1), (1, 0), (1, 1), (1, 3), (1, 2), (2, 1), (0, 2), (2, 0), (2, 2))
BACK = 6
PEERS = len(OFFSETS)
TREES = (
    {0: (-1, 1), 2: (0, 2), 1: (2, 3), 4: (2, 3), 5: (2, 3), 3: (4, 4), 6: (4, 4), 7: (5, 4), 8: (5, 4)},
    {1: (-1, 1), 2: (1, 2), 3: (1, 2), 0: (2, 3), 4: (3, 3), 5: (2, 3), 6: (4, 4), 7: (5, 4), 8: (4, 4)},
)
PASSED = tuple(frozenset(p for p, _ in tree.values()) for tree in TREES)
DIRECT_X = 14
DIRECT_A = 5


def split(x):
    high = x.astype(BF16)
    return high, (x - high.astype(F32)).astype(BF16)


def dot3(a_high, a_low, b_high, b_low):
    def one(a, b):
        return jnp.dot(a, b, preferred_element_type=F32)

    return one(a_high, b_high) + (one(a_high, b_low) + one(a_low, b_high))


def corner(rows):
    lane = lax.broadcasted_iota(jnp.int32, (8, W), 1)
    sub = lax.broadcasted_iota(jnp.int32, (8, W), 0)
    first = lane[0:1]
    rows = list(rows)
    upper, inverse = [], []

    def lanes(x, c):
        return jnp.broadcast_to(x[:, c : c + 1], (8, W))

    for s in range(W // 8):
        r = 8 * s
        block = rows[s]
        c = [lanes(block, r + j) for j in range(8)]
        e = {(i, j): c[j][i : i + 1, :] for j in range(8) for i in range(j, 8)}
        inv, low = [None] * 8, {}
        for j in range(8):
            inv[j] = lax.rsqrt(e[j, j])
            for i in range(j + 1, 8):
                low[i, j] = e[i, j] * inv[j]
            for i in range(j + 1, 8):
                for m in range(j + 1, i + 1):
                    e[i, m] = e[i, m] - low[i, j] * low[m, j]
        diagonal = (lane >= r) & (lane < r + 8)
        own = jnp.where(diagonal, (lane - r == sub).astype(F32), block)
        u = []
        for j in range(8):
            t = own[j : j + 1, :]
            for m in range(j):
                t = t - low[j, m] * u[m]
            u.append(t * inv[j])
        z = [None] * 8
        for j in reversed(range(8)):
            t = u[j]
            for m in range(j + 1, 8):
                t = t - low[m, j] * z[m]
            z[j] = t * inv[j]
        solved = jnp.concatenate(u, axis=0)
        small = jnp.zeros((8, W), F32)
        for j in range(8):
            t = jnp.where(first == r + j, e[j, j] * inv[j], 0.0)
            for m in range(j + 1, 8):
                t = jnp.where(first == r + m, low[m, j], t)
            small = jnp.where(sub == j, t, small)
        upper.append(jnp.where(lane >= r + 8, solved, small))
        inverse.append(jnp.where(lane < r + 8, solved, 0.0))
        z = [jnp.broadcast_to(t, (8, W)) for t in z]
        for i in range(s + 1, W // 8):
            t = jnp.where(diagonal, 0.0, rows[i])
            for j in range(8):
                t = t - lanes(rows[i], r + j) * z[j]
            rows[i] = t
    return upper, inverse


def tile(k, j):
    return k * (2 * N + 1 - k) // 2 + j - k


def at(i, size=W):
    return pl.ds(pl.multiple_of(i * size, size), size)


def kernel(
    a, left, right, effects, separator, separator_effects, tip,
    factor, diagonal_out, coupling_out, arrow_out, tip_out,
    tiles, high, low, panel, corner_up, corner_inv, x_own, x_got, xt_high, xt_low, self_gram,
    result_got, next_got, cross_got, tip_got, tip_own, cross_own,
    tile_send, tile_recv, x_send, x_recv, result_send, result_recv,
    next_send, next_recv, cross_send, cross_recv, tip_send, tip_recv, separator_sem,
):
    me = lax.axis_index("col")
    tm = lax.axis_index("tm")
    tms = lax.axis_size("tm")
    z, y = me // 4, me % 4

    def moved(dz, dy):
        return ((z + dz + 4) % 4) * 4 + (y + dy + 4) % 4

    barrier = pltpu.get_barrier_semaphore()

    def greet(o, _):
        pl.semaphore_signal(barrier, inc=1, device_id={"tm": tm, "col": (me + o) % N}, device_id_type=MESH)
        return 0

    lax.fori_loop(1, N, greet, 0)

    def greet_tm(o, _):
        pl.semaphore_signal(barrier, inc=1, device_id={"tm": (tm + o) % tms, "col": me}, device_id_type=MESH)
        return 0

    lax.fori_loop(1, tms, greet_tm, 0)
    pl.semaphore_wait(barrier, N - 1 + tms - 1)

    def tile_copy(k, source, index, to):
        return pltpu.make_async_remote_copy(
            src_ref=tiles.at[tile(k, source)], dst_ref=tiles.at[tile(k, source)],
            send_sem=tile_send.at[k, index], recv_sem=tile_recv.at[tile(k, source)],
            device_id={"tm": tm, "col": to}, device_id_type=MESH,
        )

    def tile_arrival(k, source):
        return tile_copy(k, source, 0, (me + 1) % N)

    separator_copy = pltpu.make_async_copy(separator, diagonal_out, separator_sem)
    separator_copy.start()

    def own_tile(k, _):
        tiles[tile(k, me)] = a[at(k), :]
        return 0

    lax.fori_loop(0, me + 1, own_tile, 0)

    def direct_tiles(k, action):
        @pl.when(me >= k)
        def _():
            def to_one(o, _):
                to = ((z + o // 4) % 4) * 4 + (y + o % 4) % 4
                action(tile_copy(k, me, o - 1, to))
                return 0

            lax.fori_loop(1, N, to_one, 0)

    def start(copy):
        copy.start()

    def wait_send(copy):
        copy.wait_send()

    for k in range(DIRECT_A):
        direct_tiles(k, start)

    def along(k, first, second):
        even = 1 - k % 2
        dz = first * (1 - even) + second * even
        dy = first * even + second * (1 - even)
        return ((z + dz + 4) % 4) * 4 + (y + dy + 4) % 4

    def way(k):
        return 1 - 2 * ((k // 2) % 2)

    def wait_tile(k, source):
        @pl.when(source >= k)
        def _():
            tile_arrival(k, source).wait_recv()

    def forward(k, source, index, to, action):
        @pl.when(source >= k)
        def _():
            action(tile_copy(k, source, index, to))

    def stage_own(k, action, waits):
        forward(k, me, 0, along(k, 1, 0), action)
        forward(k, me, 1, along(k, -1, 0), action)

    def stage_next(k, action, waits):
        source = along(k, -way(k), 0)
        if waits:
            wait_tile(k, source)
        forward(k, source, 2, along(k, way(k), 0), action)

    def stage_line(k, action, waits):
        if waits:
            wait_tile(k, along(k, way(k), 0))
            wait_tile(k, along(k, 2, 0))
        for i in range(4):
            source = along(k, i, 0)
            forward(k, source, 3 + 2 * i, along(k, 0, 1), action)
            forward(k, source, 4 + 2 * i, along(k, 0, -1), action)

    def stage_last(k, action, waits):
        for i in range(4):
            source = along(k, i, -way(k))
            if waits:
                wait_tile(k, source)
            forward(k, source, 11 + i, along(k, 0, way(k)), action)

    STAGES = (stage_last, stage_line, stage_next, stage_own)

    def pass_tiles(k):
        for i, stage in enumerate(STAGES):
            ahead = k + DIRECT_A - 3 + i

            @pl.when((ahead >= DIRECT_A) & (ahead < N))
            def _():
                stage(ahead, start, True)

    def wait_tiles(k):
        @pl.when(k < DIRECT_A)
        def _():
            def one(j, _):
                @pl.when(j != me)
                def _():
                    tile_arrival(k, j).wait_recv()

                return 0

            lax.fori_loop(k, N, one, 0)

        @pl.when(k >= DIRECT_A)
        def _():
            for i in range(4):
                wait_tile(k, along(k, i, way(k)))
                wait_tile(k, along(k, i, 2))

    def clear(k, _):
        high[at(k), :] = jnp.zeros((W, B + XW), BF16)
        low[at(k), :] = jnp.zeros((W, B + XW), BF16)
        factor[at(k), :] = jnp.zeros((W, W), F32)
        return 0

    lax.fori_loop(0, N, clear, 0)

    def x_copy(d, k, parity):
        parent = TREES[parity][d][0] if parity is not None else -1
        dz, dy = OFFSETS[d]
        if parent >= 0:
            dz, dy = dz - OFFSETS[parent][0], dy - OFFSETS[parent][1]
        return pltpu.make_async_remote_copy(
            src_ref=x_own.at[at(k)] if parent < 0 else x_got.at[parent * N + k],
            dst_ref=x_got.at[d * N + k],
            send_sem=x_send.at[d * N + k], recv_sem=x_recv.at[d * N + k],
            device_id={"tm": tm, "col": moved(dz, dy)}, device_id_type=MESH,
        )

    def pass_x(k, level):
        for parity in range(2):

            @pl.when((k >= 0) & (k < DIRECT_X) & (k % 2 == parity))
            def _():
                tree = TREES[parity]
                for d, (_, hops) in tree.items():
                    if hops == level - 1 and d in PASSED[parity]:
                        x_copy(d, k, parity).wait_recv()
                for d, (_, hops) in tree.items():
                    if hops == level:
                        x_copy(d, k, parity).start()

    def step(k, half):
        rows = half * W
        part_rows = pl.ds(pl.multiple_of(rows, W), W)
        pass_tiles(k)
        wait_tiles(k)

        def subtract(j, _):
            panel[part_rows, at(j)] = tiles[tile(k, j)] - panel[part_rows, at(j)]
            return 0

        lax.fori_loop(k, N, subtract, 0)
        panel[part_rows, X0 : X0 + W] = left[at(k), :] - panel[part_rows, X0 : X0 + W]
        panel[part_rows, X0 + W : X0 + 2 * W] = right[at(k), :] - panel[part_rows, X0 + W : X0 + 2 * W]
        turned_rows = jnp.concatenate([effects[:, at(k)], jnp.zeros((W - NF, W), F32)], axis=0).T
        panel[part_rows, X0 + 2 * W :] = turned_rows - panel[part_rows, X0 + 2 * W :]

        upper, inverse = corner(
            [panel[pl.ds(pl.multiple_of(rows + 8 * i, 8), 8), at(k)] for i in range(W // 8)]
        )
        for i in range(W // 8):
            corner_up[8 * i : 8 * i + 8, :] = upper[i]
            corner_inv[8 * i : 8 * i + 8, :] = inverse[i]

        @pl.when(me == k)
        def _():
            factor[at(k), :] = corner_up[...].T

        inv_high, inv_low = split(corner_inv[...])

        def solve_four(c, _):
            begin = pl.multiple_of(c * 4 * W, 4 * W)
            part = dot3(inv_high, inv_low, *split(panel[part_rows, pl.ds(begin, 4 * W)]))
            for i in range(4):
                j = c * 4 + i

                @pl.when(j > k)
                def _():
                    one = part[:, i * W : (i + 1) * W]
                    high[at(k), at(j)], low[at(k), at(j)] = split(one)
                    turned = one.T
                    high[at(j), at(k)], low[at(j), at(k)] = split(turned)

                    @pl.when(me == k)
                    def _():
                        factor[at(j), :] = turned

            return 0

        lax.fori_loop(k // 4, N // 4, solve_four, 0)
        part = dot3(inv_high, inv_low, *split(panel[part_rows, X0:]))
        x_own[at(k), :] = part[:, : 2 * W]
        high[at(k), X0:], low[at(k), X0:] = split(part)

        pass_x(k, 1)

        @pl.when(k >= DIRECT_X)
        def _():
            for d in range(PEERS):
                x_copy(d, k, None).start()

        for level in range(2, 5):
            pass_x(k - level + 1, level)

        for i in range(3):
            cols = slice(i * W, (i + 1) * W)
            xt_high[cols, at(k)], xt_low[cols, at(k)] = split(part[:, cols].T)

        @pl.when(half == 0)
        def _():
            last_high, last_low = high[at(k + 1), at(k)], low[at(k + 1), at(k)]

            def update_four(c, _):
                cols = pl.ds(pl.multiple_of(c * 4 * W, 4 * W), 4 * W)
                panel[W:, cols] += dot3(last_high, last_low, high[at(k), cols], low[at(k), cols])
                return 0

            lax.fori_loop(k // 4, N // 4, update_four, 0)
            panel[W:, X0:] += dot3(last_high, last_low, high[at(k), X0:], low[at(k), X0:])

    def two_steps(p, _):
        def total(begin, width):
            def add(kk, sum_):
                return sum_ + dot3(
                    high[at(p, 2 * W), at(kk, 2 * W)], low[at(p, 2 * W), at(kk, 2 * W)],
                    high[at(kk, 2 * W), pl.ds(begin, width)], low[at(kk, 2 * W), pl.ds(begin, width)],
                )

            panel[:, pl.ds(begin, width)] = lax.fori_loop(0, p, add, jnp.zeros((2 * W, width), F32))

        def update_two(c, _):
            total(pl.multiple_of(c * 2 * W, 2 * W), 2 * W)
            return 0

        lax.fori_loop(p, N // 2, update_two, 0)
        total(X0, XW)

        def one_step(half, _):
            step(2 * p + half, half)
            return 0

        lax.fori_loop(0, 2, one_step, 0)
        return 0

    lax.fori_loop(0, N // 2, two_steps, 0)
    pass_x(DIRECT_X - 1, 4)

    for k in range(DIRECT_A):
        direct_tiles(k, wait_send)

    def drain_tiles(k, _):
        for stage in STAGES:
            stage(k, wait_send, False)
        return 0

    lax.fori_loop(DIRECT_A, N, drain_tiles, 0)

    self_gram[...] = jnp.zeros((XW, XW), F32)

    def clear_gram(i, _):
        tiles[i] = jnp.zeros((W, W), F32)
        return 0

    lax.fori_loop(0, 4 * PEERS, clear_gram, 0)

    def gram_step(p, _):
        pair = at(p, 2 * W)
        self_gram[...] += dot3(xt_high[:, pair], xt_low[:, pair], high[pair, X0:], low[pair, X0:])
        for d in range(PEERS):
            for half in range(2):
                if d in PASSED[half]:

                    @pl.when(2 * p >= DIRECT_X)
                    def _():
                        x_copy(d, 2 * p + half, None).wait_recv()
                else:
                    x_copy(d, 2 * p + half, None).wait_recv()
            got = x_got[pl.ds(d * N + 2 * p, 2)].reshape(2 * W, 2 * W)
            part = dot3(xt_high[: 2 * W, pair], xt_low[: 2 * W, pair], *split(got))
            tiles[4 * d] += part[:W, :W]
            tiles[4 * d + 1] += part[:W, W:]
            tiles[4 * d + 2] += part[W:, W:]
            tiles[4 * d + 3] += part[W:, :W]
        return 0

    lax.fori_loop(0, N // 2, gram_step, 0)

    def result_copy(d):
        dz, dy = OFFSETS[d]
        return pltpu.make_async_remote_copy(
            src_ref=tiles.at[pl.ds(4 * d, 3)], dst_ref=result_got.at[d],
            send_sem=result_send.at[d], recv_sem=result_recv.at[d],
            device_id={"tm": tm, "col": moved(-dz, -dy)}, device_id_type=MESH,
        )

    for d in range(BACK):
        result_copy(d).start()

    cross_own[...] = self_gram[2 * W : 2 * W + NF, :W]
    tip_own[...] = self_gram[2 * W : 2 * W + NF, 2 * W :]

    def tip_copy(o):
        return pltpu.make_async_remote_copy(
            src_ref=tip_own, dst_ref=tip_got.at[o],
            send_sem=tip_send.at[o], recv_sem=tip_recv.at[o],
            device_id={"tm": (tm + o) % tms, "col": me}, device_id_type=MESH,
        )

    for o in range(1, tms):
        tip_copy(o).start()

    back = {"tm": (tm + tms - 1) % tms, "col": me}
    cross_copy = pltpu.make_async_remote_copy(
        src_ref=cross_own, dst_ref=cross_got, send_sem=cross_send, recv_sem=cross_recv,
        device_id=back, device_id_type=MESH,
    )

    @pl.when(tm > 0)
    def _():
        cross_copy.start()

    separator_copy.wait()
    base = 4 * PEERS

    def next_copy(b):
        return pltpu.make_async_remote_copy(
            src_ref=tiles.at[base + b], dst_ref=next_got.at[b],
            send_sem=next_send.at[b], recv_sem=next_recv.at[b],
            device_id=back, device_id_type=MESH,
        )

    def block_out(b, left_gram, cross_gram, right_gram):
        tiles[base + b] = left_gram

        @pl.when(tm > 0)
        def _():
            next_copy(b).start()

        coupling_out[at(b), :] = -cross_gram
        diagonal_out[at(b), :] -= right_gram

    block_out(me, self_gram[:W, :W], self_gram[:W, W : 2 * W], self_gram[W : 2 * W, W : 2 * W])
    for d in range(PEERS):
        dz, dy = OFFSETS[d]
        block_out(moved(-dz, -dy), tiles[4 * d].T, tiles[4 * d + 3].T, tiles[4 * d + 2].T)
    for d in range(BACK):
        result_copy(d).wait_recv()
        block_out(moved(*OFFSETS[d]), result_got[d, 0], result_got[d, 1], result_got[d, 2])

    total = self_gram[2 * W : 2 * W + NF, 2 * W :]
    for o in range(1, tms):
        tip_copy(o).wait_recv()
        total = total + tip_got[o]
    tip_out[...] = tip[...] - total[:, :NF]

    arrow_out[...] = separator_effects[...] - self_gram[2 * W : 2 * W + NF, W : 2 * W]

    @pl.when(tm < tms - 1)
    def _():
        cross_copy.wait_recv()
        arrow_out[...] -= cross_got[...]

        def add_next(b, _):
            next_copy(b).wait_recv()
            diagonal_out[at(b), :] -= next_got[b]
            return 0

        lax.fori_loop(0, N, add_next, 0)

    for d in range(PEERS):

        def drain_x(k, _):
            x_copy(d, k, None).wait_send()
            return 0

        lax.fori_loop(0, N, drain_x, 0)
    for d in range(BACK):
        result_copy(d).wait_send()
    for o in range(1, tms):
        tip_copy(o).wait_send()

    @pl.when(tm > 0)
    def _():
        cross_copy.wait_send()

        def drain_next(b, _):
            next_copy(b).wait_send()
            return 0

        lax.fori_loop(0, N, drain_next, 0)


def local(interior, left, right, effects, separator, separator_effects, tip):
    tms = lax.axis_size("tm")
    dma = pltpu.SemaphoreType.DMA
    copies = PEERS * N
    vmem = pl.BlockSpec(memory_space=pltpu.VMEM)
    outputs = pl.pallas_call(
        kernel,
        out_shape=(
            jax.ShapeDtypeStruct((B, W), F32),
            jax.ShapeDtypeStruct((B, W), F32),
            jax.ShapeDtypeStruct((B, W), F32),
            jax.ShapeDtypeStruct((NF, W), F32),
            jax.ShapeDtypeStruct((NF, NF), F32),
        ),
        in_specs=[vmem] * 4 + [pl.BlockSpec(memory_space=pl.ANY)] + [vmem] * 2,
        out_specs=[vmem] * 5,
        scratch_shapes=[
            pltpu.VMEM((TILES, W, W), F32),
            pltpu.VMEM((B, B + XW), BF16),
            pltpu.VMEM((B, B + XW), BF16),
            pltpu.VMEM((2 * W, B + XW), F32),
            pltpu.VMEM((W, W), F32),
            pltpu.VMEM((W, W), F32),
            pltpu.VMEM((B, 2 * W), F32),
            pltpu.VMEM((copies, W, 2 * W), F32),
            pltpu.VMEM((XW, B), BF16),
            pltpu.VMEM((XW, B), BF16),
            pltpu.VMEM((XW, XW), F32),
            pltpu.VMEM((BACK, 3, W, W), F32),
            pltpu.VMEM((N, W, W), F32),
            pltpu.VMEM((NF, W), F32),
            pltpu.VMEM((8, NF, W), F32),
            pltpu.VMEM((NF, W), F32),
            pltpu.VMEM((NF, W), F32),
            dma((N, N)),
            dma((TILES,)),
            dma((copies,)),
            dma((copies,)),
            dma((BACK,)),
            dma((BACK,)),
            dma((N,)),
            dma((N,)),
            dma(()),
            dma(()),
            dma((8,)),
            dma((8,)),
            dma(()),
        ],
        compiler_params=pltpu.CompilerParams(
            collective_id=0, has_side_effects=True, vmem_limit_bytes=64 * 1024 * 1024 - 65536
        ),
        name="eliminate",
    )(interior[0], left[0], right[0], effects[0], separator[0], separator_effects[0], tip)
    return tuple(x[None] for x in outputs[:4]) + (outputs[4],)


def solution(mesh):
    return jax.shard_map(
        local,
        mesh=mesh,
        in_specs=(
            P("tm", None, "col"),
            P("tm", None, "col"),
            P("tm", None, "col"),
            P("tm", None, None),
            P("tm", None, "col"),
            P("tm", None, "col"),
            P(),
        ),
        out_specs=(
            P("tm", None, "col"),
            P("tm", None, "col"),
            P("tm", None, "col"),
            P("tm", None, "col"),
            P(),
        ),
        check_vma=False,
    )
```

```python
import jax
import jax.numpy as jnp
from jax import lax
from jax.experimental import pallas as pl
from jax.experimental.pallas import tpu as pltpu
from jax.sharding import PartitionSpec as P

W = 128
N = 16
B = N * W
NF = 64
X0 = B
XW = 3 * W
TILES = N * (N + 1) // 2
MESH = pl.DeviceIdType.MESH
F32, BF16 = jnp.float32, jnp.bfloat16
OFFSETS = ((0, 1), (1, 0), (1, 1), (1, 3), (1, 2), (2, 1), (0, 2), (2, 0), (2, 2))
BACK = 6
PEERS = len(OFFSETS)
TREES = (
    {0: (-1, 1), 2: (0, 2), 1: (2, 3), 4: (2, 3), 5: (2, 3), 3: (4, 4), 6: (4, 4), 7: (5, 4), 8: (5, 4)},
    {1: (-1, 1), 2: (1, 2), 3: (1, 2), 0: (2, 3), 4: (3, 3), 5: (2, 3), 6: (4, 4), 7: (5, 4), 8: (4, 4)},
)
PASSED = tuple(frozenset(p for p, _ in tree.values()) for tree in TREES)
DIRECT_X = 14
DIRECT_A = 1


def split(x):
    high = x.astype(BF16)
    return high, (x - high.astype(F32)).astype(BF16)


def dot3(a_high, a_low, b_high, b_low):
    def one(a, b):
        return jnp.dot(a, b, preferred_element_type=F32)

    return one(a_high, b_high) + (one(a_high, b_low) + one(a_low, b_high))


def corner(rows):
    lane = lax.broadcasted_iota(jnp.int32, (8, W), 1)
    sub = lax.broadcasted_iota(jnp.int32, (8, W), 0)
    first = lane[0:1]
    rows = list(rows)
    upper, inverse = [], []

    def lanes(x, c):
        return jnp.broadcast_to(x[:, c : c + 1], (8, W))

    for s in range(W // 8):
        r = 8 * s
        block = rows[s]
        c = [lanes(block, r + j) for j in range(8)]
        e = {(i, j): c[j][i : i + 1, :] for j in range(8) for i in range(j, 8)}
        inv, low = [None] * 8, {}
        for j in range(8):
            inv[j] = lax.rsqrt(e[j, j])
            for i in range(j + 1, 8):
                low[i, j] = e[i, j] * inv[j]
            for i in range(j + 1, 8):
                for m in range(j + 1, i + 1):
                    e[i, m] = e[i, m] - low[i, j] * low[m, j]
        diagonal = (lane >= r) & (lane < r + 8)
        own = jnp.where(diagonal, (lane - r == sub).astype(F32), block)
        u = []
        for j in range(8):
            t = own[j : j + 1, :]
            for m in range(j):
                t = t - low[j, m] * u[m]
            u.append(t * inv[j])
        z = [None] * 8
        for j in reversed(range(8)):
            t = u[j]
            for m in range(j + 1, 8):
                t = t - low[m, j] * z[m]
            z[j] = t * inv[j]
        solved = jnp.concatenate(u, axis=0)
        small = jnp.zeros((8, W), F32)
        for j in range(8):
            t = jnp.where(first == r + j, e[j, j] * inv[j], 0.0)
            for m in range(j + 1, 8):
                t = jnp.where(first == r + m, low[m, j], t)
            small = jnp.where(sub == j, t, small)
        upper.append(jnp.where(lane >= r + 8, solved, small))
        inverse.append(jnp.where(lane < r + 8, solved, 0.0))
        z = [jnp.broadcast_to(t, (8, W)) for t in z]
        for i in range(s + 1, W // 8):
            t = jnp.where(diagonal, 0.0, rows[i])
            for j in range(8):
                t = t - lanes(rows[i], r + j) * z[j]
            rows[i] = t
    return upper, inverse


def tile(k, j):
    return k * (2 * N + 1 - k) // 2 + j - k


def at(i, size=W):
    return pl.ds(pl.multiple_of(i * size, size), size)


def kernel(
    a, left, right, effects, separator, separator_effects, tip,
    factor, diagonal_out, coupling_out, arrow_out, tip_out,
    tiles, high, low, panel, corner_up, corner_inv, x_own, x_got, xt_high, xt_low, self_gram,
    result_got, next_got, cross_got, tip_got, tip_own, cross_own,
    tile_send, tile_recv, x_send, x_recv, result_send, result_recv,
    next_send, next_recv, cross_send, cross_recv, tip_send, tip_recv, separator_sem,
):
    me = lax.axis_index("col")
    tm = lax.axis_index("tm")
    tms = lax.axis_size("tm")
    z, y = me // 4, me % 4

    def moved(dz, dy):
        return ((z + dz + 4) % 4) * 4 + (y + dy + 4) % 4

    barrier = pltpu.get_barrier_semaphore()

    def greet(o, _):
        pl.semaphore_signal(barrier, inc=1, device_id={"tm": tm, "col": (me + o) % N}, device_id_type=MESH)
        return 0

    lax.fori_loop(1, N, greet, 0)

    def greet_tm(o, _):
        pl.semaphore_signal(barrier, inc=1, device_id={"tm": (tm + o) % tms, "col": me}, device_id_type=MESH)
        return 0

    lax.fori_loop(1, tms, greet_tm, 0)
    pl.semaphore_wait(barrier, N - 1 + tms - 1)

    def tile_copy(k, source, index, to):
        return pltpu.make_async_remote_copy(
            src_ref=tiles.at[tile(k, source)], dst_ref=tiles.at[tile(k, source)],
            send_sem=tile_send.at[k, index], recv_sem=tile_recv.at[tile(k, source)],
            device_id={"tm": tm, "col": to}, device_id_type=MESH,
        )

    def tile_arrival(k, source):
        return tile_copy(k, source, 0, (me + 1) % N)

    separator_copy = pltpu.make_async_copy(separator, diagonal_out, separator_sem)
    separator_copy.start()

    def own_tile(k, _):
        tiles[tile(k, me)] = a[at(k), :]
        return 0

    lax.fori_loop(0, me + 1, own_tile, 0)

    def direct_tiles(k, action):
        @pl.when(me >= k)
        def _():
            def to_one(o, _):
                to = ((z + o // 4) % 4) * 4 + (y + o % 4) % 4
                action(tile_copy(k, me, o - 1, to))
                return 0

            lax.fori_loop(1, N, to_one, 0)

    def start(copy):
        copy.start()

    def wait_send(copy):
        copy.wait_send()

    def along(k, first, second):
        even = 1 - k % 2
        dz = first * (1 - even) + second * even
        dy = first * even + second * (1 - even)
        return ((z + dz + 4) % 4) * 4 + (y + dy + 4) % 4

    def way(k):
        return 1 - 2 * ((k // 2) % 2)

    def wait_tile(k, source):
        @pl.when(source >= k)
        def _():
            tile_arrival(k, source).wait_recv()

    def forward(k, source, index, to, action):
        @pl.when(source >= k)
        def _():
            action(tile_copy(k, source, index, to))

    def stage_own(k, action, waits):
        forward(k, me, 0, along(k, 1, 0), action)
        forward(k, me, 1, along(k, -1, 0), action)

    def stage_next(k, action, waits):
        source = along(k, -way(k), 0)
        if waits:
            wait_tile(k, source)
        forward(k, source, 2, along(k, way(k), 0), action)

    def stage_line(k, action, waits):
        if waits:
            wait_tile(k, along(k, way(k), 0))
            wait_tile(k, along(k, 2, 0))
        for i in range(4):
            source = along(k, i, 0)
            forward(k, source, 3 + 2 * i, along(k, 0, 1), action)
            forward(k, source, 4 + 2 * i, along(k, 0, -1), action)

    def stage_last(k, action, waits):
        for i in range(4):
            source = along(k, i, -way(k))
            if waits:
                wait_tile(k, source)
            forward(k, source, 11 + i, along(k, 0, way(k)), action)

    STAGES = (stage_last, stage_line, stage_next, stage_own)

    for k in range(DIRECT_A, DIRECT_A + 3):
        stage_own(k, start, True)
    for k in range(DIRECT_A):
        direct_tiles(k, start)

    def pass_tiles(k):
        for i, stage in enumerate(STAGES):

            @pl.when(k + 1 + i < N)
            def _():
                stage(k + 1 + i, start, True)

    def wait_tiles(k):
        @pl.when(k < DIRECT_A)
        def _():
            def one(j, _):
                @pl.when(j != me)
                def _():
                    tile_arrival(k, j).wait_recv()

                return 0

            lax.fori_loop(k, N, one, 0)

        @pl.when(k >= DIRECT_A)
        def _():
            for i in range(4):
                wait_tile(k, along(k, i, way(k)))
                wait_tile(k, along(k, i, 2))

    def clear(k, _):
        high[at(k), :] = jnp.zeros((W, B + XW), BF16)
        low[at(k), :] = jnp.zeros((W, B + XW), BF16)
        factor[at(k), :] = jnp.zeros((W, W), F32)
        return 0

    lax.fori_loop(0, N, clear, 0)

    stage_next(DIRECT_A, start, True)
    stage_next(DIRECT_A + 1, start, True)
    stage_line(DIRECT_A, start, True)

    def x_copy(d, k, parity):
        parent = TREES[parity][d][0] if parity is not None else -1
        dz, dy = OFFSETS[d]
        if parent >= 0:
            dz, dy = dz - OFFSETS[parent][0], dy - OFFSETS[parent][1]
        return pltpu.make_async_remote_copy(
            src_ref=x_own.at[at(k)] if parent < 0 else x_got.at[parent * N + k],
            dst_ref=x_got.at[d * N + k],
            send_sem=x_send.at[d * N + k], recv_sem=x_recv.at[d * N + k],
            device_id={"tm": tm, "col": moved(dz, dy)}, device_id_type=MESH,
        )

    def pass_x(k, level):
        for parity in range(2):

            @pl.when((k >= 0) & (k < DIRECT_X) & (k % 2 == parity))
            def _():
                tree = TREES[parity]
                for d, (_, hops) in tree.items():
                    if hops == level - 1 and d in PASSED[parity]:
                        x_copy(d, k, parity).wait_recv()
                for d, (_, hops) in tree.items():
                    if hops == level:
                        x_copy(d, k, parity).start()

    def step(k, half):
        rows = half * W
        part_rows = pl.ds(pl.multiple_of(rows, W), W)
        pass_tiles(k)
        wait_tiles(k)

        def subtract(j, _):
            panel[part_rows, at(j)] = tiles[tile(k, j)] - panel[part_rows, at(j)]
            return 0

        lax.fori_loop(k, N, subtract, 0)
        panel[part_rows, X0 : X0 + W] = left[at(k), :] - panel[part_rows, X0 : X0 + W]
        panel[part_rows, X0 + W : X0 + 2 * W] = right[at(k), :] - panel[part_rows, X0 + W : X0 + 2 * W]
        turned_rows = jnp.concatenate([effects[:, at(k)], jnp.zeros((W - NF, W), F32)], axis=0).T
        panel[part_rows, X0 + 2 * W :] = turned_rows - panel[part_rows, X0 + 2 * W :]

        upper, inverse = corner(
            [panel[pl.ds(pl.multiple_of(rows + 8 * i, 8), 8), at(k)] for i in range(W // 8)]
        )
        for i in range(W // 8):
            corner_up[8 * i : 8 * i + 8, :] = upper[i]
            corner_inv[8 * i : 8 * i + 8, :] = inverse[i]

        @pl.when(me == k)
        def _():
            factor[at(k), :] = corner_up[...].T

        inv_high, inv_low = split(corner_inv[...])

        part = dot3(inv_high, inv_low, *split(panel[part_rows, X0:]))
        x_own[at(k), :] = part[:, : 2 * W]
        high[at(k), X0:], low[at(k), X0:] = split(part)

        pass_x(k, 1)

        @pl.when(k >= DIRECT_X)
        def _():
            for d in range(PEERS):
                x_copy(d, k, None).start()

        for level in range(2, 5):
            pass_x(k - level + 1, level)

        def solve_four(c, _):
            begin = pl.multiple_of(c * 4 * W, 4 * W)
            part = dot3(inv_high, inv_low, *split(panel[part_rows, pl.ds(begin, 4 * W)]))
            for i in range(4):
                j = c * 4 + i

                @pl.when(j > k)
                def _():
                    one = part[:, i * W : (i + 1) * W]
                    high[at(k), at(j)], low[at(k), at(j)] = split(one)
                    turned = one.T
                    high[at(j), at(k)], low[at(j), at(k)] = split(turned)

                    @pl.when(me == k)
                    def _():
                        factor[at(j), :] = turned

            return 0

        lax.fori_loop((k + 1) // 4, N // 4, solve_four, 0)
        for i in range(3):
            cols = slice(i * W, (i + 1) * W)
            xt_high[cols, at(k)], xt_low[cols, at(k)] = split(part[:, cols].T)

        @pl.when(half == 0)
        def _():
            last_high, last_low = high[at(k + 1), at(k)], low[at(k + 1), at(k)]

            def update_four(c, _):
                cols = pl.ds(pl.multiple_of(c * 4 * W, 4 * W), 4 * W)
                panel[W:, cols] += dot3(last_high, last_low, high[at(k), cols], low[at(k), cols])
                return 0

            lax.fori_loop(k // 4, N // 4, update_four, 0)
            panel[W:, X0:] += dot3(last_high, last_low, high[at(k), X0:], low[at(k), X0:])

    def two_steps(p, _):
        def total(begin, width):
            def add(kk, sum_):
                return sum_ + dot3(
                    high[at(p, 2 * W), at(kk, 2 * W)], low[at(p, 2 * W), at(kk, 2 * W)],
                    high[at(kk, 2 * W), pl.ds(begin, width)], low[at(kk, 2 * W), pl.ds(begin, width)],
                )

            panel[:, pl.ds(begin, width)] = lax.fori_loop(0, p, add, jnp.zeros((2 * W, width), F32))

        def update_two(c, _):
            total(pl.multiple_of(c * 2 * W, 2 * W), 2 * W)
            return 0

        lax.fori_loop(p, N // 2, update_two, 0)
        total(X0, XW)

        def one_step(half, _):
            step(2 * p + half, half)
            return 0

        lax.fori_loop(0, 2, one_step, 0)
        return 0

    lax.fori_loop(0, N // 2, two_steps, 0)
    pass_x(DIRECT_X - 1, 4)

    for k in range(DIRECT_A):
        direct_tiles(k, wait_send)

    def drain_tiles(k, _):
        for stage in STAGES:
            stage(k, wait_send, False)
        return 0

    lax.fori_loop(DIRECT_A, N, drain_tiles, 0)

    self_gram[...] = jnp.zeros((XW, XW), F32)

    def clear_gram(i, _):
        tiles[i] = jnp.zeros((W, W), F32)
        return 0

    lax.fori_loop(0, 4 * PEERS, clear_gram, 0)

    def gram_step(p, _):
        pair = at(p, 2 * W)
        self_gram[...] += dot3(xt_high[:, pair], xt_low[:, pair], high[pair, X0:], low[pair, X0:])
        for d in range(PEERS):
            for half in range(2):
                if d in PASSED[half]:

                    @pl.when(2 * p >= DIRECT_X)
                    def _():
                        x_copy(d, 2 * p + half, None).wait_recv()
                else:
                    x_copy(d, 2 * p + half, None).wait_recv()
            got = x_got[pl.ds(d * N + 2 * p, 2)].reshape(2 * W, 2 * W)
            part = dot3(xt_high[: 2 * W, pair], xt_low[: 2 * W, pair], *split(got))
            tiles[4 * d] += part[:W, :W]
            tiles[4 * d + 1] += part[:W, W:]
            tiles[4 * d + 2] += part[W:, W:]
            tiles[4 * d + 3] += part[W:, :W]
        return 0

    lax.fori_loop(0, N // 2, gram_step, 0)

    def result_copy(d):
        dz, dy = OFFSETS[d]
        return pltpu.make_async_remote_copy(
            src_ref=tiles.at[pl.ds(4 * d, 3)], dst_ref=result_got.at[d],
            send_sem=result_send.at[d], recv_sem=result_recv.at[d],
            device_id={"tm": tm, "col": moved(-dz, -dy)}, device_id_type=MESH,
        )

    for d in range(BACK):
        result_copy(d).start()

    cross_own[...] = self_gram[2 * W : 2 * W + NF, :W]
    tip_own[...] = self_gram[2 * W : 2 * W + NF, 2 * W :]

    def tip_copy(o):
        return pltpu.make_async_remote_copy(
            src_ref=tip_own, dst_ref=tip_got.at[o],
            send_sem=tip_send.at[o], recv_sem=tip_recv.at[o],
            device_id={"tm": (tm + o) % tms, "col": me}, device_id_type=MESH,
        )

    for o in range(1, tms):
        tip_copy(o).start()

    back = {"tm": (tm + tms - 1) % tms, "col": me}
    cross_copy = pltpu.make_async_remote_copy(
        src_ref=cross_own, dst_ref=cross_got, send_sem=cross_send, recv_sem=cross_recv,
        device_id=back, device_id_type=MESH,
    )

    @pl.when(tm > 0)
    def _():
        cross_copy.start()

    separator_copy.wait()
    base = 4 * PEERS

    def next_copy(b):
        return pltpu.make_async_remote_copy(
            src_ref=tiles.at[base + b], dst_ref=next_got.at[b],
            send_sem=next_send.at[b], recv_sem=next_recv.at[b],
            device_id=back, device_id_type=MESH,
        )

    def block_out(b, left_gram, cross_gram, right_gram):
        tiles[base + b] = left_gram

        @pl.when(tm > 0)
        def _():
            next_copy(b).start()

        coupling_out[at(b), :] = -cross_gram
        diagonal_out[at(b), :] -= right_gram

    block_out(me, self_gram[:W, :W], self_gram[:W, W : 2 * W], self_gram[W : 2 * W, W : 2 * W])
    for d in range(PEERS):
        dz, dy = OFFSETS[d]
        block_out(moved(-dz, -dy), tiles[4 * d].T, tiles[4 * d + 3].T, tiles[4 * d + 2].T)
    for d in range(BACK):
        result_copy(d).wait_recv()
        block_out(moved(*OFFSETS[d]), result_got[d, 0], result_got[d, 1], result_got[d, 2])

    total = self_gram[2 * W : 2 * W + NF, 2 * W :]
    for o in range(1, tms):
        tip_copy(o).wait_recv()
        total = total + tip_got[o]
    tip_out[...] = tip[...] - total[:, :NF]

    arrow_out[...] = separator_effects[...] - self_gram[2 * W : 2 * W + NF, W : 2 * W]

    @pl.when(tm < tms - 1)
    def _():
        cross_copy.wait_recv()
        arrow_out[...] -= cross_got[...]

        def add_next(b, _):
            next_copy(b).wait_recv()
            diagonal_out[at(b), :] -= next_got[b]
            return 0

        lax.fori_loop(0, N, add_next, 0)

    for d in range(PEERS):

        def drain_x(k, _):
            x_copy(d, k, None).wait_send()
            return 0

        lax.fori_loop(0, N, drain_x, 0)
    for d in range(BACK):
        result_copy(d).wait_send()
    for o in range(1, tms):
        tip_copy(o).wait_send()

    @pl.when(tm > 0)
    def _():
        cross_copy.wait_send()

        def drain_next(b, _):
            next_copy(b).wait_send()
            return 0

        lax.fori_loop(0, N, drain_next, 0)


def local(interior, left, right, effects, separator, separator_effects, tip):
    tms = lax.axis_size("tm")
    dma = pltpu.SemaphoreType.DMA
    copies = PEERS * N
    vmem = pl.BlockSpec(memory_space=pltpu.VMEM)
    outputs = pl.pallas_call(
        kernel,
        out_shape=(
            jax.ShapeDtypeStruct((B, W), F32),
            jax.ShapeDtypeStruct((B, W), F32),
            jax.ShapeDtypeStruct((B, W), F32),
            jax.ShapeDtypeStruct((NF, W), F32),
            jax.ShapeDtypeStruct((NF, NF), F32),
        ),
        in_specs=[vmem] * 4 + [pl.BlockSpec(memory_space=pl.ANY)] + [vmem] * 2,
        out_specs=[vmem] * 5,
        scratch_shapes=[
            pltpu.VMEM((TILES, W, W), F32),
            pltpu.VMEM((B, B + XW), BF16),
            pltpu.VMEM((B, B + XW), BF16),
            pltpu.VMEM((2 * W, B + XW), F32),
            pltpu.VMEM((W, W), F32),
            pltpu.VMEM((W, W), F32),
            pltpu.VMEM((B, 2 * W), F32),
            pltpu.VMEM((copies, W, 2 * W), F32),
            pltpu.VMEM((XW, B), BF16),
            pltpu.VMEM((XW, B), BF16),
            pltpu.VMEM((XW, XW), F32),
            pltpu.VMEM((BACK, 3, W, W), F32),
            pltpu.VMEM((N, W, W), F32),
            pltpu.VMEM((NF, W), F32),
            pltpu.VMEM((8, NF, W), F32),
            pltpu.VMEM((NF, W), F32),
            pltpu.VMEM((NF, W), F32),
            dma((N, N)),
            dma((TILES,)),
            dma((copies,)),
            dma((copies,)),
            dma((BACK,)),
            dma((BACK,)),
            dma((N,)),
            dma((N,)),
            dma(()),
            dma(()),
            dma((8,)),
            dma((8,)),
            dma(()),
        ],
        compiler_params=pltpu.CompilerParams(
            collective_id=0, has_side_effects=True, vmem_limit_bytes=64 * 1024 * 1024 - 65536
        ),
        name="eliminate",
    )(interior[0], left[0], right[0], effects[0], separator[0], separator_effects[0], tip)
    return tuple(x[None] for x in outputs[:4]) + (outputs[4],)


def solution(mesh):
    return jax.shard_map(
        local,
        mesh=mesh,
        in_specs=(
            P("tm", None, "col"),
            P("tm", None, "col"),
            P("tm", None, "col"),
            P("tm", None, None),
            P("tm", None, "col"),
            P("tm", None, "col"),
            P(),
        ),
        out_specs=(
            P("tm", None, "col"),
            P("tm", None, "col"),
            P("tm", None, "col"),
            P("tm", None, "col"),
            P(),
        ),
        check_vma=False,
    )
```

```python
import jax
import jax.numpy as jnp
from jax import lax
from jax.experimental import pallas as pl
from jax.experimental.pallas import tpu as pltpu
from jax.sharding import PartitionSpec as P

W = 128
N = 16
B = N * W
NF = 64
X0 = B
XW = 3 * W
TILES = N * (N + 1) // 2
MESH = pl.DeviceIdType.MESH
F32, BF16 = jnp.float32, jnp.bfloat16
OFFSETS = ((0, 1), (1, 0), (1, 1), (1, 3), (1, 2), (2, 1), (0, 2), (2, 0), (2, 2))
BACK = 6
PEERS = len(OFFSETS)
TREES = (
    {0: (-1, 1), 2: (0, 2), 1: (2, 3), 4: (2, 3), 5: (2, 3), 3: (4, 4), 6: (4, 4), 7: (5, 4), 8: (5, 4)},
    {1: (-1, 1), 2: (1, 2), 3: (1, 2), 0: (2, 3), 4: (3, 3), 5: (2, 3), 6: (4, 4), 7: (5, 4), 8: (4, 4)},
)
PASSED = tuple(frozenset(p for p, _ in tree.values()) for tree in TREES)
DIRECT_A = 1


def split(x):
    high = x.astype(BF16)
    return high, (x - high.astype(F32)).astype(BF16)


def dot3(a_high, a_low, b_high, b_low):
    left = jnp.concatenate([a_high, a_high, a_low], axis=1)
    right = jnp.concatenate([b_high, b_low, b_high], axis=0)
    return jnp.dot(left, right, preferred_element_type=F32)


def corner(rows):
    lane = lax.broadcasted_iota(jnp.int32, (8, W), 1)
    sub = lax.broadcasted_iota(jnp.int32, (8, W), 0)
    first = lane[0:1]
    rows = list(rows)
    upper, inverse = [], []

    def lanes(x, c):
        return jnp.broadcast_to(x[:, c : c + 1], (8, W))

    for s in range(W // 8):
        r = 8 * s
        block = rows[s]
        c = [lanes(block, r + j) for j in range(8)]
        e = {(i, j): c[j][i : i + 1, :] for j in range(8) for i in range(j, 8)}
        inv, low = [None] * 8, {}
        for j in range(8):
            inv[j] = lax.rsqrt(e[j, j])
            for i in range(j + 1, 8):
                low[i, j] = e[i, j] * inv[j]
            for i in range(j + 1, 8):
                for m in range(j + 1, i + 1):
                    e[i, m] = e[i, m] - low[i, j] * low[m, j]
        diagonal = (lane >= r) & (lane < r + 8)
        own = jnp.where(diagonal, (lane - r == sub).astype(F32), block)
        u = []
        for j in range(8):
            t = own[j : j + 1, :]
            for m in range(j):
                t = t - low[j, m] * u[m]
            u.append(t * inv[j])
        z = [None] * 8
        for j in reversed(range(8)):
            t = u[j]
            for m in range(j + 1, 8):
                t = t - low[m, j] * z[m]
            z[j] = t * inv[j]
        solved = jnp.concatenate(u, axis=0)
        small = jnp.zeros((8, W), F32)
        for j in range(8):
            t = jnp.where(first == r + j, e[j, j] * inv[j], 0.0)
            for m in range(j + 1, 8):
                t = jnp.where(first == r + m, low[m, j], t)
            small = jnp.where(sub == j, t, small)
        upper.append(jnp.where(lane >= r + 8, solved, small))
        inverse.append(jnp.where(lane < r + 8, solved, 0.0))
        z = [jnp.broadcast_to(t, (8, W)) for t in z]
        for i in range(s + 1, W // 8):
            t = jnp.where(diagonal, 0.0, rows[i])
            for j in range(8):
                t = t - lanes(rows[i], r + j) * z[j]
            rows[i] = t
    return upper, inverse


def tile(k, j):
    return k * (2 * N + 1 - k) // 2 + j - k


def at(i, size=W):
    return pl.ds(pl.multiple_of(i * size, size), size)


def kernel(
    a, left, right, effects, separator, separator_effects, tip,
    factor, diagonal_out, coupling_out, arrow_out, tip_out,
    tiles, high, low, panel, corner_up, corner_inv, x_own, x_got, xt_high, xt_low, self_gram,
    result_got, next_got, cross_got, tip_got, tip_own, cross_own,
    tile_send, tile_recv, x_send, x_recv, result_send, result_recv,
    next_send, next_recv, cross_send, cross_recv, tip_send, tip_recv, separator_sem,
):
    me = lax.axis_index("col")
    tm = lax.axis_index("tm")
    tms = lax.axis_size("tm")
    z, y = me // 4, me % 4

    def moved(dz, dy):
        return ((z + dz + 4) % 4) * 4 + (y + dy + 4) % 4

    barrier = pltpu.get_barrier_semaphore()

    def greet(o, _):
        pl.semaphore_signal(barrier, inc=1, device_id={"tm": tm, "col": (me + o) % N}, device_id_type=MESH)
        return 0

    lax.fori_loop(1, N, greet, 0)

    def greet_tm(o, _):
        pl.semaphore_signal(barrier, inc=1, device_id={"tm": (tm + o) % tms, "col": me}, device_id_type=MESH)
        return 0

    lax.fori_loop(1, tms, greet_tm, 0)
    pl.semaphore_wait(barrier, N - 1 + tms - 1)

    def tile_copy(k, source, index, to):
        return pltpu.make_async_remote_copy(
            src_ref=tiles.at[tile(k, source)], dst_ref=tiles.at[tile(k, source)],
            send_sem=tile_send.at[k, index], recv_sem=tile_recv.at[tile(k, source)],
            device_id={"tm": tm, "col": to}, device_id_type=MESH,
        )

    def tile_arrival(k, source):
        return tile_copy(k, source, 0, (me + 1) % N)

    separator_copy = pltpu.make_async_copy(separator, diagonal_out, separator_sem)
    separator_copy.start()

    def own_tile(k, _):
        tiles[tile(k, me)] = a[at(k), :]
        return 0

    lax.fori_loop(0, me + 1, own_tile, 0)

    def direct_tiles(k, action):
        @pl.when(me >= k)
        def _():
            def to_one(o, _):
                to = ((z + o // 4) % 4) * 4 + (y + o % 4) % 4
                action(tile_copy(k, me, o - 1, to))
                return 0

            lax.fori_loop(1, N, to_one, 0)

    def start(copy):
        copy.start()

    def wait_send(copy):
        copy.wait_send()

    def along(k, first, second):
        even = 1 - k % 2
        dz = first * (1 - even) + second * even
        dy = first * even + second * (1 - even)
        return ((z + dz + 4) % 4) * 4 + (y + dy + 4) % 4

    def way(k):
        return 1 - 2 * ((k // 2) % 2)

    def wait_tile(k, source):
        @pl.when(source >= k)
        def _():
            tile_arrival(k, source).wait_recv()

    def forward(k, source, index, to, action):
        @pl.when(source >= k)
        def _():
            action(tile_copy(k, source, index, to))

    def stage_own(k, action, waits):
        forward(k, me, 0, along(k, 1, 0), action)
        forward(k, me, 1, along(k, -1, 0), action)

    def stage_next(k, action, waits):
        source = along(k, -way(k), 0)
        if waits:
            wait_tile(k, source)
        forward(k, source, 2, along(k, way(k), 0), action)

    def stage_line(k, action, waits):
        if waits:
            wait_tile(k, along(k, way(k), 0))
            wait_tile(k, along(k, 2, 0))
        for i in range(4):
            source = along(k, i, 0)
            forward(k, source, 3 + 2 * i, along(k, 0, 1), action)
            forward(k, source, 4 + 2 * i, along(k, 0, -1), action)

    def stage_last(k, action, waits):
        for i in range(4):
            source = along(k, i, -way(k))
            if waits:
                wait_tile(k, source)
            forward(k, source, 11 + i, along(k, 0, way(k)), action)

    STAGES = (stage_last, stage_line, stage_next, stage_own)

    for k in range(DIRECT_A, DIRECT_A + 3):
        stage_own(k, start, True)
    for k in range(DIRECT_A):
        direct_tiles(k, start)

    def pass_tiles(k):
        for i, stage in enumerate(STAGES):

            @pl.when(k + 1 + i < N)
            def _():
                stage(k + 1 + i, start, True)

    def wait_tiles(k):
        @pl.when(k < DIRECT_A)
        def _():
            def one(j, _):
                @pl.when(j != me)
                def _():
                    tile_arrival(k, j).wait_recv()

                return 0

            lax.fori_loop(k, N, one, 0)

        @pl.when(k >= DIRECT_A)
        def _():
            for i in range(4):
                wait_tile(k, along(k, i, way(k)))
                wait_tile(k, along(k, i, 2))

    def clear(k, _):
        high[at(k), :] = jnp.zeros((W, B + XW), BF16)
        low[at(k), :] = jnp.zeros((W, B + XW), BF16)
        factor[at(k), :] = jnp.zeros((W, W), F32)
        return 0

    lax.fori_loop(0, N, clear, 0)

    stage_next(DIRECT_A, start, True)
    stage_next(DIRECT_A + 1, start, True)
    stage_line(DIRECT_A, start, True)

    def x_copy(d, k, parity):
        parent = TREES[parity][d][0] if parity is not None else -1
        dz, dy = OFFSETS[d]
        if parent >= 0:
            dz, dy = dz - OFFSETS[parent][0], dy - OFFSETS[parent][1]
        return pltpu.make_async_remote_copy(
            src_ref=x_own.at[at(k)] if parent < 0 else x_got.at[parent * N + k],
            dst_ref=x_got.at[d * N + k],
            send_sem=x_send.at[d * N + k], recv_sem=x_recv.at[d * N + k],
            device_id={"tm": tm, "col": moved(dz, dy)}, device_id_type=MESH,
        )

    def pass_x(k, level):
        for parity in range(2):

            @pl.when((k >= 0) & (k < N) & (k % 2 == parity))
            def _():
                tree = TREES[parity]
                for d, (_, hops) in tree.items():
                    if hops == level - 1 and d in PASSED[parity]:
                        x_copy(d, k, parity).wait_recv()
                for d, (_, hops) in tree.items():
                    if hops == level:
                        x_copy(d, k, parity).start()

    def step(k, half):
        rows = half * W
        part_rows = pl.ds(pl.multiple_of(rows, W), W)
        pass_tiles(k)
        wait_tiles(k)

        def subtract(j, _):
            panel[part_rows, at(j)] = tiles[tile(k, j)] - panel[part_rows, at(j)]
            return 0

        lax.fori_loop(k, N, subtract, 0)
        panel[part_rows, X0 : X0 + W] = left[at(k), :] - panel[part_rows, X0 : X0 + W]
        panel[part_rows, X0 + W : X0 + 2 * W] = right[at(k), :] - panel[part_rows, X0 + W : X0 + 2 * W]
        turned_rows = jnp.concatenate([effects[:, at(k)], jnp.zeros((W - NF, W), F32)], axis=0).T
        panel[part_rows, X0 + 2 * W :] = turned_rows - panel[part_rows, X0 + 2 * W :]

        upper, inverse = corner(
            [panel[pl.ds(pl.multiple_of(rows + 8 * i, 8), 8), at(k)] for i in range(W // 8)]
        )
        for i in range(W // 8):
            corner_up[8 * i : 8 * i + 8, :] = upper[i]
            corner_inv[8 * i : 8 * i + 8, :] = inverse[i]

        @pl.when(me == k)
        def _():
            factor[at(k), :] = corner_up[...].T

        inv_high, inv_low = split(corner_inv[...])

        part = dot3(inv_high, inv_low, *split(panel[part_rows, X0:]))
        x_own[at(k), :] = part[:, : 2 * W]
        high[at(k), X0:], low[at(k), X0:] = split(part)

        pass_x(k, 1)

        for level in range(2, 5):
            pass_x(k - level + 1, level)

        def solve_four(c, _):
            begin = pl.multiple_of(c * 4 * W, 4 * W)
            part = dot3(inv_high, inv_low, *split(panel[part_rows, pl.ds(begin, 4 * W)]))
            for i in range(4):
                j = c * 4 + i

                @pl.when(j > k)
                def _():
                    one = part[:, i * W : (i + 1) * W]
                    high[at(k), at(j)], low[at(k), at(j)] = split(one)
                    turned = one.T
                    high[at(j), at(k)], low[at(j), at(k)] = split(turned)

                    @pl.when(me == k)
                    def _():
                        factor[at(j), :] = turned

            return 0

        lax.fori_loop((k + 1) // 4, N // 4, solve_four, 0)
        for i in range(3):
            cols = slice(i * W, (i + 1) * W)
            xt_high[cols, at(k)], xt_low[cols, at(k)] = split(part[:, cols].T)

        @pl.when(half == 0)
        def _():
            last_high, last_low = high[at(k + 1), at(k)], low[at(k + 1), at(k)]

            def update_four(c, _):
                cols = pl.ds(pl.multiple_of(c * 4 * W, 4 * W), 4 * W)
                panel[W:, cols] += dot3(last_high, last_low, high[at(k), cols], low[at(k), cols])
                return 0

            lax.fori_loop(k // 4, N // 4, update_four, 0)
            panel[W:, X0:] += dot3(last_high, last_low, high[at(k), X0:], low[at(k), X0:])

    def two_steps(p, _):
        def total(begin, width):
            def add(kk, sum_):
                return sum_ + dot3(
                    high[at(p, 2 * W), at(kk, 2 * W)], low[at(p, 2 * W), at(kk, 2 * W)],
                    high[at(kk, 2 * W), pl.ds(begin, width)], low[at(kk, 2 * W), pl.ds(begin, width)],
                )

            panel[:, pl.ds(begin, width)] = lax.fori_loop(0, p, add, jnp.zeros((2 * W, width), F32))

        def update_two(c, _):
            total(pl.multiple_of(c * 2 * W, 2 * W), 2 * W)
            return 0

        lax.fori_loop(p, N // 2, update_two, 0)
        total(X0, XW)

        def one_step(half, _):
            step(2 * p + half, half)
            return 0

        lax.fori_loop(0, 2, one_step, 0)
        return 0

    lax.fori_loop(0, N // 2, two_steps, 0)

    for k in range(DIRECT_A):
        direct_tiles(k, wait_send)

    def drain_tiles(k, _):
        for stage in STAGES:
            stage(k, wait_send, False)
        return 0

    lax.fori_loop(DIRECT_A, N, drain_tiles, 0)

    self_gram[...] = jnp.zeros((XW, XW), F32)

    def clear_gram(i, _):
        tiles[i] = jnp.zeros((W, W), F32)
        return 0

    lax.fori_loop(0, 4 * PEERS, clear_gram, 0)

    def gram_step(p, _):
        pair = at(p, 2 * W)
        self_gram[...] += dot3(xt_high[:, pair], xt_low[:, pair], high[pair, X0:], low[pair, X0:])
        for d in range(PEERS):
            for half in range(2):
                if d not in PASSED[half]:
                    x_copy(d, 2 * p + half, None).wait_recv()
            got = x_got[pl.ds(d * N + 2 * p, 2)].reshape(2 * W, 2 * W)
            part = dot3(xt_high[: 2 * W, pair], xt_low[: 2 * W, pair], *split(got))
            tiles[4 * d] += part[:W, :W]
            tiles[4 * d + 1] += part[:W, W:]
            tiles[4 * d + 2] += part[W:, W:]
            tiles[4 * d + 3] += part[W:, :W]
        return 0

    lax.fori_loop(0, 2, gram_step, 0)
    for level in range(2, 5):
        pass_x(N - level + 1, level)
    lax.fori_loop(2, 4, gram_step, 0)
    for level in range(3, 5):
        pass_x(N - level + 2, level)
    lax.fori_loop(4, 6, gram_step, 0)
    pass_x(N - 1, 4)
    lax.fori_loop(6, N // 2, gram_step, 0)

    def result_copy(d):
        dz, dy = OFFSETS[d]
        return pltpu.make_async_remote_copy(
            src_ref=tiles.at[pl.ds(4 * d, 3)], dst_ref=result_got.at[d],
            send_sem=result_send.at[d], recv_sem=result_recv.at[d],
            device_id={"tm": tm, "col": moved(-dz, -dy)}, device_id_type=MESH,
        )

    for d in range(BACK):
        result_copy(d).start()

    cross_own[...] = self_gram[2 * W : 2 * W + NF, :W]
    tip_own[...] = self_gram[2 * W : 2 * W + NF, 2 * W :]

    def tip_copy(o):
        return pltpu.make_async_remote_copy(
            src_ref=tip_own, dst_ref=tip_got.at[o],
            send_sem=tip_send.at[o], recv_sem=tip_recv.at[o],
            device_id={"tm": (tm + o) % tms, "col": me}, device_id_type=MESH,
        )

    for o in range(1, tms):
        tip_copy(o).start()

    back = {"tm": (tm + tms - 1) % tms, "col": me}
    cross_copy = pltpu.make_async_remote_copy(
        src_ref=cross_own, dst_ref=cross_got, send_sem=cross_send, recv_sem=cross_recv,
        device_id=back, device_id_type=MESH,
    )

    @pl.when(tm > 0)
    def _():
        cross_copy.start()

    separator_copy.wait()
    base = 4 * PEERS

    def next_copy(b):
        return pltpu.make_async_remote_copy(
            src_ref=tiles.at[base + b], dst_ref=next_got.at[b],
            send_sem=next_send.at[b], recv_sem=next_recv.at[b],
            device_id=back, device_id_type=MESH,
        )

    def block_out(b, left_gram, cross_gram, right_gram):
        tiles[base + b] = left_gram

        @pl.when(tm > 0)
        def _():
            next_copy(b).start()

        coupling_out[at(b), :] = -cross_gram
        diagonal_out[at(b), :] -= right_gram

    block_out(me, self_gram[:W, :W], self_gram[:W, W : 2 * W], self_gram[W : 2 * W, W : 2 * W])
    for d in range(PEERS):
        dz, dy = OFFSETS[d]
        block_out(moved(-dz, -dy), tiles[4 * d].T, tiles[4 * d + 3].T, tiles[4 * d + 2].T)
    for d in range(BACK):
        result_copy(d).wait_recv()
        block_out(moved(*OFFSETS[d]), result_got[d, 0], result_got[d, 1], result_got[d, 2])

    total = self_gram[2 * W : 2 * W + NF, 2 * W :]
    for o in range(1, tms):
        tip_copy(o).wait_recv()
        total = total + tip_got[o]
    tip_out[...] = tip[...] - total[:, :NF]

    arrow_out[...] = separator_effects[...] - self_gram[2 * W : 2 * W + NF, W : 2 * W]

    @pl.when(tm < tms - 1)
    def _():
        cross_copy.wait_recv()
        arrow_out[...] -= cross_got[...]

        def add_next(b, _):
            next_copy(b).wait_recv()
            diagonal_out[at(b), :] -= next_got[b]
            return 0

        lax.fori_loop(0, N, add_next, 0)

    for d in range(PEERS):

        def drain_x(k, _):
            x_copy(d, k, None).wait_send()
            return 0

        lax.fori_loop(0, N, drain_x, 0)
    for d in range(BACK):
        result_copy(d).wait_send()
    for o in range(1, tms):
        tip_copy(o).wait_send()

    @pl.when(tm > 0)
    def _():
        cross_copy.wait_send()

        def drain_next(b, _):
            next_copy(b).wait_send()
            return 0

        lax.fori_loop(0, N, drain_next, 0)


def local(interior, left, right, effects, separator, separator_effects, tip):
    tms = lax.axis_size("tm")
    dma = pltpu.SemaphoreType.DMA
    copies = PEERS * N
    vmem = pl.BlockSpec(memory_space=pltpu.VMEM)
    outputs = pl.pallas_call(
        kernel,
        out_shape=(
            jax.ShapeDtypeStruct((B, W), F32),
            jax.ShapeDtypeStruct((B, W), F32),
            jax.ShapeDtypeStruct((B, W), F32),
            jax.ShapeDtypeStruct((NF, W), F32),
            jax.ShapeDtypeStruct((NF, NF), F32),
        ),
        in_specs=[vmem] * 4 + [pl.BlockSpec(memory_space=pl.ANY)] + [vmem] * 2,
        out_specs=[vmem] * 5,
        scratch_shapes=[
            pltpu.VMEM((TILES, W, W), F32),
            pltpu.VMEM((B, B + XW), BF16),
            pltpu.VMEM((B, B + XW), BF16),
            pltpu.VMEM((2 * W, B + XW), F32),
            pltpu.VMEM((W, W), F32),
            pltpu.VMEM((W, W), F32),
            pltpu.VMEM((B, 2 * W), F32),
            pltpu.VMEM((copies, W, 2 * W), F32),
            pltpu.VMEM((XW, B), BF16),
            pltpu.VMEM((XW, B), BF16),
            pltpu.VMEM((XW, XW), F32),
            pltpu.VMEM((BACK, 3, W, W), F32),
            pltpu.VMEM((N, W, W), F32),
            pltpu.VMEM((NF, W), F32),
            pltpu.VMEM((8, NF, W), F32),
            pltpu.VMEM((NF, W), F32),
            pltpu.VMEM((NF, W), F32),
            dma((N, N)),
            dma((TILES,)),
            dma((copies,)),
            dma((copies,)),
            dma((BACK,)),
            dma((BACK,)),
            dma((N,)),
            dma((N,)),
            dma(()),
            dma(()),
            dma((8,)),
            dma((8,)),
            dma(()),
        ],
        compiler_params=pltpu.CompilerParams(
            collective_id=0, has_side_effects=True, vmem_limit_bytes=64 * 1024 * 1024 - 65536
        ),
        name="eliminate",
    )(interior[0], left[0], right[0], effects[0], separator[0], separator_effects[0], tip)
    return tuple(x[None] for x in outputs[:4]) + (outputs[4],)


def solution(mesh):
    return jax.shard_map(
        local,
        mesh=mesh,
        in_specs=(
            P("tm", None, "col"),
            P("tm", None, "col"),
            P("tm", None, "col"),
            P("tm", None, None),
            P("tm", None, "col"),
            P("tm", None, "col"),
            P(),
        ),
        out_specs=(
            P("tm", None, "col"),
            P("tm", None, "col"),
            P("tm", None, "col"),
            P("tm", None, "col"),
            P(),
        ),
        check_vma=False,
    )
```

```python
import jax
import jax.numpy as jnp
from jax import lax
from jax.experimental import pallas as pl
from jax.experimental.pallas import tpu as pltpu
from jax.sharding import PartitionSpec as P

W = 128
N = 16
B = N * W
NF = 64
X0 = B
XW = 3 * W
TILES = N * (N + 1) // 2
MESH = pl.DeviceIdType.MESH
F32, BF16 = jnp.float32, jnp.bfloat16
OFFSETS = ((0, 1), (1, 0), (1, 1), (1, 3), (1, 2), (2, 1), (0, 2), (2, 0), (2, 2))
BACK = 6
PEERS = len(OFFSETS)
TREES = (
    {0: (-1, 1), 2: (0, 2), 1: (2, 3), 4: (2, 3), 5: (2, 3), 3: (4, 4), 6: (4, 4), 7: (5, 4), 8: (5, 4)},
    {1: (-1, 1), 2: (1, 2), 3: (1, 2), 0: (2, 3), 4: (3, 3), 5: (2, 3), 6: (4, 4), 7: (5, 4), 8: (4, 4)},
)
PASSED = tuple(frozenset(p for p, _ in tree.values()) for tree in TREES)


def split(x):
    high = x.astype(BF16)
    return high, (x - high.astype(F32)).astype(BF16)


def dot3(a_high, a_low, b_high, b_low):
    left = jnp.concatenate([a_high, a_high, a_low], axis=1)
    right = jnp.concatenate([b_high, b_low, b_high], axis=0)
    return jnp.dot(left, right, preferred_element_type=F32)


def corner(rows):
    lane = lax.broadcasted_iota(jnp.int32, (8, W), 1)
    sub = lax.broadcasted_iota(jnp.int32, (8, W), 0)
    first = lane[0:1]
    rows = list(rows)
    upper, inverse = [], []

    def lanes(x, c):
        return jnp.broadcast_to(x[:, c : c + 1], (8, W))

    for s in range(W // 8):
        r = 8 * s
        block = rows[s]
        c = [lanes(block, r + j) for j in range(8)]
        e = {(i, j): c[j][i : i + 1, :] for j in range(8) for i in range(j, 8)}
        inv, low = [None] * 8, {}
        for j in range(8):
            inv[j] = lax.rsqrt(e[j, j])
            for i in range(j + 1, 8):
                low[i, j] = e[i, j] * inv[j]
            for i in range(j + 1, 8):
                for m in range(j + 1, i + 1):
                    e[i, m] = e[i, m] - low[i, j] * low[m, j]
        diagonal = (lane >= r) & (lane < r + 8)
        own = jnp.where(diagonal, (lane - r == sub).astype(F32), block)
        u = []
        for j in range(8):
            t = own[j : j + 1, :]
            for m in range(j):
                t = t - low[j, m] * u[m]
            u.append(t * inv[j])
        z = [None] * 8
        for j in reversed(range(8)):
            t = u[j]
            for m in range(j + 1, 8):
                t = t - low[m, j] * z[m]
            z[j] = t * inv[j]
        solved = jnp.concatenate(u, axis=0)
        small = jnp.zeros((8, W), F32)
        for j in range(8):
            t = jnp.where(first == r + j, e[j, j] * inv[j], 0.0)
            for m in range(j + 1, 8):
                t = jnp.where(first == r + m, low[m, j], t)
            small = jnp.where(sub == j, t, small)
        upper.append(jnp.where(lane >= r + 8, solved, small))
        inverse.append(jnp.where(lane < r + 8, solved, 0.0))
        z = [jnp.broadcast_to(t, (8, W)) for t in z]
        for i in range(s + 1, W // 8):
            t = jnp.where(diagonal, 0.0, rows[i])
            for j in range(8):
                t = t - lanes(rows[i], r + j) * z[j]
            rows[i] = t
    return upper, inverse


def tile(k, j):
    return k * (2 * N + 1 - k) // 2 + j - k


def at(i, size=W):
    return pl.ds(pl.multiple_of(i * size, size), size)


def kernel(
    a, left, right, effects, separator, separator_effects, tip,
    factor, diagonal_out, coupling_out, arrow_out, tip_out,
    tiles, high, low, panel, corner_up, corner_inv, x_own, x_got, xt_high, xt_low, self_gram,
    result_got, next_got, cross_got, tip_got, tip_own, cross_own,
    tile_send, tile_recv, x_send, x_recv, result_send, result_recv,
    next_send, next_recv, cross_send, cross_recv, tip_send, tip_recv, separator_sem,
):
    me = lax.axis_index("col")
    tm = lax.axis_index("tm")
    tms = lax.axis_size("tm")
    z, y = me // 4, me % 4

    def moved(dz, dy):
        return ((z + dz + 4) % 4) * 4 + (y + dy + 4) % 4

    barrier = pltpu.get_barrier_semaphore()

    def greet(o, _):
        pl.semaphore_signal(barrier, inc=1, device_id={"tm": tm, "col": (me + o) % N}, device_id_type=MESH)
        return 0

    lax.fori_loop(1, N, greet, 0)

    def greet_tm(o, _):
        pl.semaphore_signal(barrier, inc=1, device_id={"tm": (tm + o) % tms, "col": me}, device_id_type=MESH)
        return 0

    lax.fori_loop(1, tms, greet_tm, 0)
    pl.semaphore_wait(barrier, N - 1 + tms - 1)

    def tile_copy(k, source, index, to):
        return pltpu.make_async_remote_copy(
            src_ref=tiles.at[tile(k, source)], dst_ref=tiles.at[tile(k, source)],
            send_sem=tile_send.at[k, index], recv_sem=tile_recv.at[tile(k, source)],
            device_id={"tm": tm, "col": to}, device_id_type=MESH,
        )

    def tile_arrival(k, source):
        return tile_copy(k, source, 0, (me + 1) % N)

    separator_copy = pltpu.make_async_copy(separator, diagonal_out, separator_sem)
    separator_copy.start()

    def own_tile(k, _):
        tiles[tile(k, me)] = a[at(k), :]
        return 0

    lax.fori_loop(0, me + 1, own_tile, 0)

    def start(copy):
        copy.start()

    def wait_send(copy):
        copy.wait_send()

    def along(k, first, second):
        even = 1 - k % 2
        dz = first * (1 - even) + second * even
        dy = first * even + second * (1 - even)
        return ((z + dz + 4) % 4) * 4 + (y + dy + 4) % 4

    def way(k):
        return 1 - 2 * ((k // 2) % 2)

    def wait_tile(k, source):
        @pl.when(source >= k)
        def _():
            tile_arrival(k, source).wait_recv()

    def forward(k, source, index, to, action):
        @pl.when(source >= k)
        def _():
            action(tile_copy(k, source, index, to))

    def stage_own(k, action, waits):
        forward(k, me, 0, along(k, 1, 0), action)
        forward(k, me, 1, along(k, -1, 0), action)

    def stage_next(k, action, waits):
        source = along(k, -way(k), 0)
        if waits:
            wait_tile(k, source)
        forward(k, source, 2, along(k, way(k), 0), action)

    def stage_line(k, action, waits):
        if waits:
            wait_tile(k, along(k, way(k), 0))
            wait_tile(k, along(k, 2, 0))
        for i in range(4):
            source = along(k, i, 0)
            forward(k, source, 3 + 2 * i, along(k, 0, 1), action)
            forward(k, source, 4 + 2 * i, along(k, 0, -1), action)

    def stage_last(k, action, waits):
        for i in range(4):
            source = along(k, i, -way(k))
            if waits:
                wait_tile(k, source)
            forward(k, source, 11 + i, along(k, 0, way(k)), action)

    STAGES = (stage_last, stage_line, stage_next, stage_own)

    for k in range(4):
        stage_own(k, start, True)

    def pass_tiles(k):
        for i, stage in enumerate(STAGES):

            @pl.when(k + 1 + i < N)
            def _():
                stage(k + 1 + i, start, True)

    def wait_tiles(k):
        for i in range(4):
            wait_tile(k, along(k, i, way(k)))
            wait_tile(k, along(k, i, 2))

    def clear(k, _):
        high[at(k), :] = jnp.zeros((W, B + XW), BF16)
        low[at(k), :] = jnp.zeros((W, B + XW), BF16)
        factor[at(k), :] = jnp.zeros((W, W), F32)
        return 0

    lax.fori_loop(0, N, clear, 0)

    for stage, panels in ((stage_next, 3), (stage_line, 2), (stage_last, 1)):
        for k in range(panels):
            stage(k, start, True)

    def x_copy(d, k, parity):
        parent = TREES[parity][d][0] if parity is not None else -1
        dz, dy = OFFSETS[d]
        if parent >= 0:
            dz, dy = dz - OFFSETS[parent][0], dy - OFFSETS[parent][1]
        return pltpu.make_async_remote_copy(
            src_ref=x_own.at[at(k)] if parent < 0 else x_got.at[parent * N + k],
            dst_ref=x_got.at[d * N + k],
            send_sem=x_send.at[d * N + k], recv_sem=x_recv.at[d * N + k],
            device_id={"tm": tm, "col": moved(dz, dy)}, device_id_type=MESH,
        )

    def pass_x(k, level):
        for parity in range(2):

            @pl.when((k >= 0) & (k < N) & (k % 2 == parity))
            def _():
                tree = TREES[parity]
                for d, (_, hops) in tree.items():
                    if hops == level - 1 and d in PASSED[parity]:
                        x_copy(d, k, parity).wait_recv()
                for d, (_, hops) in tree.items():
                    if hops == level:
                        x_copy(d, k, parity).start()

    def step(k, half):
        rows = half * W
        part_rows = pl.ds(pl.multiple_of(rows, W), W)
        pass_tiles(k)
        wait_tiles(k)

        def subtract(j, _):
            panel[part_rows, at(j)] = tiles[tile(k, j)] - panel[part_rows, at(j)]
            return 0

        lax.fori_loop(k, N, subtract, 0)
        panel[part_rows, X0 : X0 + W] = left[at(k), :] - panel[part_rows, X0 : X0 + W]
        panel[part_rows, X0 + W : X0 + 2 * W] = right[at(k), :] - panel[part_rows, X0 + W : X0 + 2 * W]
        turned_rows = jnp.concatenate([effects[:, at(k)], jnp.zeros((W - NF, W), F32)], axis=0).T
        panel[part_rows, X0 + 2 * W :] = turned_rows - panel[part_rows, X0 + 2 * W :]

        upper, inverse = corner(
            [panel[pl.ds(pl.multiple_of(rows + 8 * i, 8), 8), at(k)] for i in range(W // 8)]
        )
        for i in range(W // 8):
            corner_up[8 * i : 8 * i + 8, :] = upper[i]
            corner_inv[8 * i : 8 * i + 8, :] = inverse[i]

        @pl.when(me == k)
        def _():
            factor[at(k), :] = corner_up[...].T

        inv_high, inv_low = split(corner_inv[...])

        part = dot3(inv_high, inv_low, *split(panel[part_rows, X0:]))
        x_own[at(k), :] = part[:, : 2 * W]
        high[at(k), X0:], low[at(k), X0:] = split(part)

        pass_x(k, 1)

        for level in range(2, 5):
            pass_x(k - level + 1, level)

        def solve_four(c, _):
            begin = pl.multiple_of(c * 4 * W, 4 * W)
            part = dot3(inv_high, inv_low, *split(panel[part_rows, pl.ds(begin, 4 * W)]))
            for i in range(4):
                j = c * 4 + i

                @pl.when(j > k)
                def _():
                    one = part[:, i * W : (i + 1) * W]
                    high[at(k), at(j)], low[at(k), at(j)] = split(one)
                    turned = one.T
                    high[at(j), at(k)], low[at(j), at(k)] = split(turned)

                    @pl.when(me == k)
                    def _():
                        factor[at(j), :] = turned

            return 0

        lax.fori_loop((k + 1) // 4, N // 4, solve_four, 0)
        for i in range(3):
            cols = slice(i * W, (i + 1) * W)
            xt_high[cols, at(k)], xt_low[cols, at(k)] = split(part[:, cols].T)

        @pl.when(half == 0)
        def _():
            last_high, last_low = high[at(k + 1), at(k)], low[at(k + 1), at(k)]

            def update_four(c, _):
                cols = pl.ds(pl.multiple_of(c * 4 * W, 4 * W), 4 * W)
                panel[W:, cols] += dot3(last_high, last_low, high[at(k), cols], low[at(k), cols])
                return 0

            lax.fori_loop(k // 4, N // 4, update_four, 0)
            panel[W:, X0:] += dot3(last_high, last_low, high[at(k), X0:], low[at(k), X0:])

    def two_steps(p, _):
        def total(begin, width):
            def add(kk, sum_):
                return sum_ + dot3(
                    high[at(p, 2 * W), at(kk, 2 * W)], low[at(p, 2 * W), at(kk, 2 * W)],
                    high[at(kk, 2 * W), pl.ds(begin, width)], low[at(kk, 2 * W), pl.ds(begin, width)],
                )

            panel[:, pl.ds(begin, width)] = lax.fori_loop(0, p, add, jnp.zeros((2 * W, width), F32))

        def update_two(c, _):
            total(pl.multiple_of(c * 2 * W, 2 * W), 2 * W)
            return 0

        lax.fori_loop(p, N // 2, update_two, 0)
        total(X0, XW)

        def one_step(half, _):
            step(2 * p + half, half)
            return 0

        lax.fori_loop(0, 2, one_step, 0)
        return 0

    lax.fori_loop(0, N // 2, two_steps, 0)

    def drain_tiles(k, _):
        for stage in STAGES:
            stage(k, wait_send, False)
        return 0

    lax.fori_loop(0, N, drain_tiles, 0)

    self_gram[...] = jnp.zeros((XW, XW), F32)

    def clear_gram(i, _):
        tiles[i] = jnp.zeros((W, W), F32)
        return 0

    lax.fori_loop(0, 4 * PEERS, clear_gram, 0)

    def gram_step(p, _):
        pair = at(p, 2 * W)
        self_gram[...] += dot3(xt_high[:, pair], xt_low[:, pair], high[pair, X0:], low[pair, X0:])
        for d in range(PEERS):
            for half in range(2):
                if d not in PASSED[half]:
                    x_copy(d, 2 * p + half, None).wait_recv()
            got = x_got[pl.ds(d * N + 2 * p, 2)].reshape(2 * W, 2 * W)
            part = dot3(xt_high[: 2 * W, pair], xt_low[: 2 * W, pair], *split(got))
            tiles[4 * d] += part[:W, :W]
            tiles[4 * d + 1] += part[:W, W:]
            tiles[4 * d + 2] += part[W:, W:]
            tiles[4 * d + 3] += part[W:, :W]
        return 0

    lax.fori_loop(0, 2, gram_step, 0)
    for level in range(2, 5):
        pass_x(N - level + 1, level)
    lax.fori_loop(2, 4, gram_step, 0)
    for level in range(3, 5):
        pass_x(N - level + 2, level)
    lax.fori_loop(4, 6, gram_step, 0)
    pass_x(N - 1, 4)
    lax.fori_loop(6, N // 2, gram_step, 0)

    def result_copy(d):
        dz, dy = OFFSETS[d]
        return pltpu.make_async_remote_copy(
            src_ref=tiles.at[pl.ds(4 * d, 3)], dst_ref=result_got.at[d],
            send_sem=result_send.at[d], recv_sem=result_recv.at[d],
            device_id={"tm": tm, "col": moved(-dz, -dy)}, device_id_type=MESH,
        )

    for d in range(BACK):
        result_copy(d).start()

    cross_own[...] = self_gram[2 * W : 2 * W + NF, :W]
    tip_own[...] = self_gram[2 * W : 2 * W + NF, 2 * W :]

    def tip_copy(o):
        return pltpu.make_async_remote_copy(
            src_ref=tip_own, dst_ref=tip_got.at[o],
            send_sem=tip_send.at[o], recv_sem=tip_recv.at[o],
            device_id={"tm": (tm + o) % tms, "col": me}, device_id_type=MESH,
        )

    for o in range(1, tms):
        tip_copy(o).start()

    back = {"tm": (tm + tms - 1) % tms, "col": me}
    cross_copy = pltpu.make_async_remote_copy(
        src_ref=cross_own, dst_ref=cross_got, send_sem=cross_send, recv_sem=cross_recv,
        device_id=back, device_id_type=MESH,
    )

    @pl.when(tm > 0)
    def _():
        cross_copy.start()

    separator_copy.wait()
    base = 4 * PEERS

    def next_copy(b):
        return pltpu.make_async_remote_copy(
            src_ref=tiles.at[base + b], dst_ref=next_got.at[b],
            send_sem=next_send.at[b], recv_sem=next_recv.at[b],
            device_id=back, device_id_type=MESH,
        )

    def block_out(b, left_gram, cross_gram, right_gram):
        tiles[base + b] = left_gram

        @pl.when(tm > 0)
        def _():
            next_copy(b).start()

        coupling_out[at(b), :] = -cross_gram
        diagonal_out[at(b), :] -= right_gram

    block_out(me, self_gram[:W, :W], self_gram[:W, W : 2 * W], self_gram[W : 2 * W, W : 2 * W])
    for d in range(PEERS):
        dz, dy = OFFSETS[d]
        block_out(moved(-dz, -dy), tiles[4 * d].T, tiles[4 * d + 3].T, tiles[4 * d + 2].T)
    for d in range(BACK):
        result_copy(d).wait_recv()
        block_out(moved(*OFFSETS[d]), result_got[d, 0], result_got[d, 1], result_got[d, 2])

    total = self_gram[2 * W : 2 * W + NF, 2 * W :]
    for o in range(1, tms):
        tip_copy(o).wait_recv()
        total = total + tip_got[o]
    tip_out[...] = tip[...] - total[:, :NF]

    arrow_out[...] = separator_effects[...] - self_gram[2 * W : 2 * W + NF, W : 2 * W]

    @pl.when(tm < tms - 1)
    def _():
        cross_copy.wait_recv()
        arrow_out[...] -= cross_got[...]

        def add_next(b, _):
            next_copy(b).wait_recv()
            diagonal_out[at(b), :] -= next_got[b]
            return 0

        lax.fori_loop(0, N, add_next, 0)

    for d in range(PEERS):

        def drain_x(k, _):
            x_copy(d, k, None).wait_send()
            return 0

        lax.fori_loop(0, N, drain_x, 0)
    for d in range(BACK):
        result_copy(d).wait_send()
    for o in range(1, tms):
        tip_copy(o).wait_send()

    @pl.when(tm > 0)
    def _():
        cross_copy.wait_send()

        def drain_next(b, _):
            next_copy(b).wait_send()
            return 0

        lax.fori_loop(0, N, drain_next, 0)


def local(interior, left, right, effects, separator, separator_effects, tip):
    tms = lax.axis_size("tm")
    dma = pltpu.SemaphoreType.DMA
    copies = PEERS * N
    vmem = pl.BlockSpec(memory_space=pltpu.VMEM)
    outputs = pl.pallas_call(
        kernel,
        out_shape=(
            jax.ShapeDtypeStruct((B, W), F32),
            jax.ShapeDtypeStruct((B, W), F32),
            jax.ShapeDtypeStruct((B, W), F32),
            jax.ShapeDtypeStruct((NF, W), F32),
            jax.ShapeDtypeStruct((NF, NF), F32),
        ),
        in_specs=[vmem] * 4 + [pl.BlockSpec(memory_space=pl.ANY)] + [vmem] * 2,
        out_specs=[vmem] * 5,
        scratch_shapes=[
            pltpu.VMEM((TILES, W, W), F32),
            pltpu.VMEM((B, B + XW), BF16),
            pltpu.VMEM((B, B + XW), BF16),
            pltpu.VMEM((2 * W, B + XW), F32),
            pltpu.VMEM((W, W), F32),
            pltpu.VMEM((W, W), F32),
            pltpu.VMEM((B, 2 * W), F32),
            pltpu.VMEM((copies, W, 2 * W), F32),
            pltpu.VMEM((XW, B), BF16),
            pltpu.VMEM((XW, B), BF16),
            pltpu.VMEM((XW, XW), F32),
            pltpu.VMEM((BACK, 3, W, W), F32),
            pltpu.VMEM((N, W, W), F32),
            pltpu.VMEM((NF, W), F32),
            pltpu.VMEM((8, NF, W), F32),
            pltpu.VMEM((NF, W), F32),
            pltpu.VMEM((NF, W), F32),
            dma((N, N)),
            dma((TILES,)),
            dma((copies,)),
            dma((copies,)),
            dma((BACK,)),
            dma((BACK,)),
            dma((N,)),
            dma((N,)),
            dma(()),
            dma(()),
            dma((8,)),
            dma((8,)),
            dma(()),
        ],
        compiler_params=pltpu.CompilerParams(
            collective_id=0, has_side_effects=True, vmem_limit_bytes=64 * 1024 * 1024 - 65536
        ),
        name="eliminate",
    )(interior[0], left[0], right[0], effects[0], separator[0], separator_effects[0], tip)
    return tuple(x[None] for x in outputs[:4]) + (outputs[4],)


def solution(mesh):
    return jax.shard_map(
        local,
        mesh=mesh,
        in_specs=(
            P("tm", None, "col"),
            P("tm", None, "col"),
            P("tm", None, "col"),
            P("tm", None, None),
            P("tm", None, "col"),
            P("tm", None, "col"),
            P(),
        ),
        out_specs=(
            P("tm", None, "col"),
            P("tm", None, "col"),
            P("tm", None, "col"),
            P("tm", None, "col"),
            P(),
        ),
        check_vma=False,
    )
```
